32 devices in a mesh: seg: 8 (over y, x, core), grp: 4 (over z).
Axes of the slice: x: 2, y: 2, z: 4, core: 2. Of those that a mesh axis runs over, the one named last changes fastest.
Arguments:
- strain: bfloat16 [4096, 1792], P(('seg', 'grp')), may hold values from -40 to 40
- counts: int32 [4096], P(('seg', 'grp')), may hold values from 448 to 1792, as said below
- working: int32 [4096], P(('seg', 'grp')), may hold values 0 or 1
- mixing: bfloat16 [512, 512], P('grp'), may hold values from -0.25 to 0.25
- owners: int32 [2], replicated, may hold values from 0 to 31
- offsets: int32 [2], replicated, may hold values from 0 to 64
Outputs:
- correlations: bfloat16 [2, 201, 64, 4096], P(None, None, None, ('seg', 'grp'))
The draws below stay inside these ranges and needn't reach their ends.
Inputs may be any that keep to these rules, and one draw needn't show every extreme that they name: `counts`: some channel has 1792 valid samples in every draw.
All inputs are finite; a program needn't handle non-finite values. No bound on the sum of `working` on one device may be relied on, other than what follows from the above.
Results may differ from the reference program's by a relative error of at most 0.0058.
Values may be sent and summed in bfloat16 or wider, within the bound.
A program may use at most 64 MiB of HBM per device.

```python
import math
import jax
import jax.numpy as jnp
from jax import lax

CH_DEV = 128
NS = 1792
SRC = 64
LAG = 100
ROUNDS = 2
LAGS = 201
SEG_CH = 512
CHANNELS = 4096


def draw_strain(key, part):
    key = jax.random.fold_in(key, 7)
    base_key, channel_key, time_key = jax.random.split(key, 3)
    base = jnp.clip(jax.random.normal(base_key, (CHANNELS, NS), jnp.float32), -4.0, 4.0)
    top = 10.0
    channel_scale = 0.3 * jnp.exp(jax.random.uniform(channel_key, (CHANNELS, 1), jnp.float32, 0.0, math.log(10.0)))
    width = max(NS // 64, 1)
    pieces = NS // width
    time_scale = 0.3 * jnp.exp(jax.random.uniform(time_key, (1, pieces), jnp.float32, 0.0, math.log(top)))
    time_scale = jnp.repeat(time_scale, width, axis=1)
    return (base * channel_scale * time_scale).astype(jnp.bfloat16)


def draw_counts(key, part):
    key = jax.random.fold_in(key, 11)
    device_key, extra_key, full_key = jax.random.split(key, 3)
    devices = CHANNELS // CH_DEV
    device_weight = jax.random.randint(device_key, (devices,), 1, 5)
    extra = jax.random.randint(extra_key, (CHANNELS,), 0, NS - NS // 4 + 1)
    counts = NS // 4 + extra * jnp.repeat(device_weight, CH_DEV) // 4
    full_index = jax.random.randint(full_key, (), 0, CHANNELS)
    counts = counts.at[full_index].set(NS)
    return counts.astype(jnp.int32)


def with_ends(array, key, least, top_value):
    longest = array.shape.index(max(array.shape))
    spots = []
    for shift in (0, 1):
        where = [jax.random.randint(jax.random.fold_in(key, axis), (), 0, length) for axis, length in enumerate(array.shape)]
        where[longest] = (where[longest] + shift) % array.shape[longest]
        spots.append(tuple(where))
    return array.at[spots[0]].set(least).at[spots[1]].set(top_value)


def shard_levels(rng, extent, cuts, least, top_value):
    gain = 1.0
    for position, blocks in cuts:
        draws = jax.random.uniform(jax.random.fold_in(jax.random.fold_in(rng, 6), position), (blocks,), jnp.float32, least / len(cuts), top_value / len(cuts))
        gain = gain * jnp.repeat(jnp.exp(draws), extent[position] // blocks).reshape((-1,) + (1,) * (len(extent) - 1 - position))
    return gain


def centred(key, dims, scale, most, cuts=(), kind=jnp.bfloat16):
    array = scale * jax.random.normal(key, dims, jnp.float32)
    if cuts:
        array = array * shard_levels(key, dims, cuts, -0.22, 0.18)
    return jnp.clip(array, -most, most).astype(kind)


def setup_inputs(seed: int = 0) -> dict:
    key_list = jax.random.split(jax.random.key(seed), 7)
    strain = draw_strain(jax.random.fold_in(key_list[6], 71), 0)
    counts = draw_counts(jax.random.fold_in(key_list[6], 71), 0)
    working = with_ends((jax.random.randint(key_list[2], (CHANNELS,), 0, 16) < 15).astype(jnp.int32), jax.random.fold_in(key_list[2], 1), 0, 1)
    mixing = centred(key_list[3], (SEG_CH, SEG_CH), SEG_CH ** -0.5, 0.25, ((0, 4),))
    owners = jax.random.randint(key_list[4], (ROUNDS,), 0, CHANNELS // CH_DEV).astype(jnp.int32)
    offsets = jax.random.randint(key_list[5], (ROUNDS,), 0, CH_DEV - SRC + 1).astype(jnp.int32)
    return {"strain": strain, "counts": counts, "working": working, "mixing": mixing, "owners": owners, "offsets": offsets}


epsilon = 1e-05

def reference(strain, counts, working, mixing, owners, offsets):
    groups = CHANNELS // SEG_CH
    positions = jnp.arange(NS, dtype=jnp.int32)
    usable = (positions[None, :] < counts[:, None]) & (working[:, None] > 0)
    masked = jnp.where(usable, strain, jnp.zeros_like(strain))
    blocks = masked.reshape(groups, SEG_CH, NS)

    def couple(group_block):
        return jnp.dot(mixing, group_block, preferred_element_type=jnp.float32)
    coupled = lax.map(couple, blocks).reshape(CHANNELS, NS)
    filtered = jnp.where(usable, masked.astype(jnp.float32) - coupled, jnp.float32(0.0))
    sumsq = lax.optimization_barrier(jnp.sum(filtered * filtered, axis=1))
    spread = jnp.sqrt(sumsq / counts.astype(jnp.float32) + epsilon)
    whitened = (filtered / spread[:, None]).astype(jnp.bfloat16)
    norm_scale = 1.0 / float(NS) ** 0.5
    rounds_out = []
    for round_index in range(ROUNDS):
        start_row = (owners[round_index] * CH_DEV + offsets[round_index]).astype(jnp.int32)
        zero_index = jnp.zeros((), jnp.int32)
        source = lax.dynamic_slice(whitened, (start_row, zero_index), (SRC, NS))
        source_pad = jnp.pad(source, ((0, 0), (LAG, LAG)))

        def one_lag(lag_index):
            shifted = lax.dynamic_slice_in_dim(source_pad, lag_index, NS, 1)
            products = jnp.dot(shifted, whitened.T, preferred_element_type=jnp.float32)
            return (products * norm_scale).astype(jnp.bfloat16)
        rounds_out.append(lax.map(one_lag, jnp.arange(LAGS, dtype=jnp.int32)))
    return jnp.stack(rounds_out)
```

```python
import jax
import jax.numpy as jnp
from jax import lax
from jax.experimental import pallas as pl
from jax.experimental.pallas import tpu as pltpu
from jax.sharding import PartitionSpec as P

SRC = 64
LAG = 100
ROUNDS = 2
LAGS = 201
STEP = 10
GROUPS = LAG // STEP
PAD = 128

epsilon = 1e-05
NT = (((1,), (1,)), ((), ()))


def correlate_kernel(w_ref, s_ref, out_ref, wpad, spad, left, right):
    channels, samples = w_ref.shape
    rows = s_ref.shape[0]
    scale = 1.0 / float(samples) ** 0.5
    for pad, ref in ((wpad, w_ref), (spad, s_ref)):
        edge = jnp.zeros((ref.shape[0], PAD), ref.dtype)
        pad[:, :PAD] = edge
        pad[:, PAD + samples :] = edge
        pad[:, PAD : PAD + samples] = ref[...]
    for sign_index, sign in enumerate((1, -1)):
        for group in range(GROUPS):
            start = PAD + sign * STEP * group
            left[sign_index, group * rows : (group + 1) * rows, :] = spad[:, start : start + samples]
        for delta in range(STEP):
            start = PAD - sign * (delta + 1)
            right[sign_index * STEP + delta] = wpad[:, start : start + samples]

    centre = lax.dot_general(s_ref[...], w_ref[...], NT, preferred_element_type=jnp.float32)
    centre = (centre * scale).astype(jnp.bfloat16)
    for r in range(ROUNDS):
        out_ref[r, LAG] = centre[r * SRC : (r + 1) * SRC]

    def tile(n, carry):
        sign_index = n // (STEP // 2)
        sign = 1 - 2 * sign_index
        first = (n % (STEP // 2)) * 2
        pair = right[pl.ds(n * 2, 2)].reshape(2 * channels, samples)
        products = lax.dot_general(left[sign_index], pair, NT, preferred_element_type=jnp.float32)
        products = (products * scale).astype(jnp.bfloat16)
        for group in range(GROUPS):
            for r in range(ROUNDS):
                row = group * rows + r * SRC
                for d in range(2):
                    lag = LAG + sign * (STEP * group + first + d + 1)
                    out_ref[r, lag] = products[row : row + SRC, d * channels : (d + 1) * channels]
        return carry

    lax.fori_loop(0, STEP, tile, 0)


def correlate(whitened, sources):
    channels, samples = whitened.shape
    rows = sources.shape[0]
    return pl.pallas_call(
        correlate_kernel,
        out_shape=jax.ShapeDtypeStruct((ROUNDS, LAGS, SRC, channels), jnp.bfloat16),
        in_specs=[pl.BlockSpec(memory_space=pltpu.VMEM)] * 2,
        out_specs=pl.BlockSpec(memory_space=pltpu.VMEM),
        scratch_shapes=[
            pltpu.VMEM((channels, samples + 2 * PAD), jnp.bfloat16),
            pltpu.VMEM((rows, samples + 2 * PAD), jnp.bfloat16),
            pltpu.VMEM((2, GROUPS * rows, samples), jnp.bfloat16),
            pltpu.VMEM((2 * STEP, channels, samples), jnp.bfloat16),
        ],
        compiler_params=pltpu.CompilerParams(vmem_limit_bytes=52 * 1024 * 1024),
        cost_estimate=pl.CostEstimate(
            flops=2 * LAGS * rows * channels * samples, bytes_accessed=8 << 20, transcendentals=0
        ),
        name="correlate",
    )(whitened, sources)


def on_device(strain, counts, working, mixing, owners, offsets):
    positions = lax.broadcasted_iota(jnp.int32, strain.shape, 1)
    usable = (positions < counts[:, None]) & (working[:, None] > 0)
    masked = jnp.where(usable, strain, jnp.zeros_like(strain))
    coupled = jnp.dot(
        mixing,
        lax.all_gather(masked, "grp", axis=0, tiled=True),
        preferred_element_type=jnp.float32,
    )
    filtered = jnp.where(usable, masked.astype(jnp.float32) - coupled, jnp.float32(0.0))
    sumsq = jnp.sum(filtered * filtered, axis=1)
    spread = jnp.sqrt(sumsq / counts.astype(jnp.float32) + epsilon)
    whitened = (filtered / spread[:, None]).astype(jnp.bfloat16)
    me = lax.axis_index(("seg", "grp"))
    mine = [
        jnp.where(me == owners[r], lax.dynamic_slice_in_dim(whitened, offsets[r], SRC, 0), 0)
        for r in range(ROUNDS)
    ]
    sources = lax.psum(jnp.concatenate(mine, axis=0).astype(jnp.bfloat16), ("seg", "grp"))
    return correlate(whitened, sources)


def solution(mesh):
    in_specs = (
        P(("seg", "grp"), None),
        P(("seg", "grp")),
        P(("seg", "grp")),
        P("grp", None),
        P(),
        P(),
    )
    out_specs = P(None, None, None, ("seg", "grp"))
    return jax.shard_map(
        on_device, mesh=mesh, in_specs=in_specs, out_specs=out_specs, check_vma=False
    )
```

```python
import jax
import jax.numpy as jnp
from jax import lax
from jax.experimental import pallas as pl
from jax.experimental.pallas import tpu as pltpu
from jax.sharding import PartitionSpec as P

SRC = 64
LAG = 100
ROUNDS = 2
LAGS = 201
STEP = 10
GROUPS = LAG // STEP
PAD = 128

epsilon = 1e-05
NT = (((1,), (1,)), ((), ()))


def correlate_kernel(w_ref, s_ref, out_ref, wpad, spad, left, right):
    channels, samples = w_ref.shape
    rows = s_ref.shape[0]
    scale = 1.0 / float(samples) ** 0.5
    for pad, ref in ((wpad, w_ref), (spad, s_ref)):
        edge = jnp.zeros((ref.shape[0], PAD), ref.dtype)
        pad[:, :PAD] = edge
        pad[:, PAD + samples :] = edge
        pad[:, PAD : PAD + samples] = ref[...]
    for sign_index, sign in enumerate((1, -1)):
        for group in range(GROUPS):
            start = PAD + sign * STEP * group
            left[sign_index, group * rows : (group + 1) * rows, :] = spad[:, start : start + samples]
        for delta in range(STEP):
            start = PAD - sign * (delta + 1)
            right[sign_index * STEP + delta] = wpad[:, start : start + samples]

    centre = lax.dot_general(s_ref[...], w_ref[...], NT, preferred_element_type=jnp.float32)
    centre = (centre * scale).astype(jnp.bfloat16)
    for r in range(ROUNDS):
        out_ref[r, LAG] = centre[r * SRC : (r + 1) * SRC]

    def tile(n, carry):
        sign_index = n // (STEP // 2)
        sign = 1 - 2 * sign_index
        first = (n % (STEP // 2)) * 2
        pair = right[pl.ds(n * 2, 2)].reshape(2 * channels, samples)
        products = lax.dot_general(left[sign_index], pair, NT, preferred_element_type=jnp.float32)
        products = (products * scale).astype(jnp.bfloat16)
        for group in range(GROUPS):
            for r in range(ROUNDS):
                row = group * rows + r * SRC
                for d in range(2):
                    lag = LAG + sign * (STEP * group + first + d + 1)
                    out_ref[r, lag] = products[row : row + SRC, d * channels : (d + 1) * channels]
        return carry

    lax.fori_loop(0, STEP, tile, 0)


def correlate(whitened, sources):
    channels, samples = whitened.shape
    rows = sources.shape[0]
    return pl.pallas_call(
        correlate_kernel,
        out_shape=jax.ShapeDtypeStruct((ROUNDS, LAGS, SRC, channels), jnp.bfloat16),
        in_specs=[pl.BlockSpec(memory_space=pltpu.VMEM)] * 2,
        out_specs=pl.BlockSpec(memory_space=pltpu.VMEM),
        scratch_shapes=[
            pltpu.VMEM((channels, samples + 2 * PAD), jnp.bfloat16),
            pltpu.VMEM((rows, samples + 2 * PAD), jnp.bfloat16),
            pltpu.VMEM((2, GROUPS * rows, samples), jnp.bfloat16),
            pltpu.VMEM((2 * STEP, channels, samples), jnp.bfloat16),
        ],
        compiler_params=pltpu.CompilerParams(vmem_limit_bytes=52 * 1024 * 1024),
        cost_estimate=pl.CostEstimate(
            flops=2 * LAGS * rows * channels * samples, bytes_accessed=8 << 20, transcendentals=0
        ),
        name="correlate",
    )(whitened, sources)


CHUNKS = 7
META = 16
XI, XE, EX, FE, SA, SB, SC, SE = range(8)
MESH = pl.DeviceIdType.MESH


def counts_column(meta, n):
    lanes = meta[0:1, :n].astype(jnp.float32) * 8.0 + meta[1:2, :n].astype(jnp.float32)
    row = lax.broadcasted_iota(jnp.int32, (n, n), 0)
    lane = lax.broadcasted_iota(jnp.int32, (n, n), 1)
    return jnp.sum(jnp.where(row == lane, lanes, 0.0), axis=1, keepdims=True)


def gather_kernel(strain, mext, msel, pick, w_out, s_out, xall, fown, fe, sa, ra, sb, rb, sc, rc,
                  s_all, mext_end, msel_end, msel_sum, msel_far, left, send, recv, msend, mrecv):
    n, samples = strain.shape
    width = samples // CHUNKS
    seg = lax.axis_index("seg")
    z = lax.axis_index("grp")
    is_end = (z % 3) == 0
    near = 1 + z // 3
    end = 3 * (z - 1)
    far = 3 - z
    far_end = 3 - end
    flips = [seg + 1 - 2 * (seg % 2), seg + 2 - 4 * ((seg // 2) % 2), seg + 4 - 8 * (seg // 4)]

    def cols(c):
        return pl.ds(c * width, width)

    def copy(src, dst, kind, c, device):
        return pltpu.make_async_remote_copy(
            src_ref=src, dst_ref=dst, send_sem=send.at[kind, c], recv_sem=recv.at[kind, c],
            device_id=device, device_id_type=MESH)

    def block(index, c):
        return xall.at[pl.ds(index * n, n), cols(c)]

    def x_copy(index, kind, c, target):
        return copy(block(index, c), block(index, c), kind, c, {"grp": target})

    def part_copy(src, dst, kind, c, device):
        return copy(src.at[:, cols(c)], dst.at[:, cols(c)], kind, c, device)

    def m_copy(src, dst, index, target):
        return pltpu.make_async_remote_copy(
            src_ref=src, dst_ref=dst, send_sem=msend.at[index], recv_sem=mrecv.at[index],
            device_id={"grp": target}, device_id_type=MESH)

    barrier = pltpu.get_barrier_semaphore()
    own_counts = counts_column(mext[n:], n)

    def usable(counts, c):
        position = lax.broadcasted_iota(jnp.int32, (n, width), 1) + c * width
        return position.astype(jnp.float32) < counts

    def mask_own(c):
        part = jnp.where(usable(own_counts, c), strain[:, c * width : (c + 1) * width].astype(jnp.float32), 0.0)
        xall[pl.ds(z * n, n), c * width : (c + 1) * width] = part.astype(jnp.bfloat16)

    def whiten(out, ref, counts):
        total = jnp.zeros((n, 1), jnp.float32)
        for c in range(CHUNKS):
            part = ref[:n, c * width : (c + 1) * width].astype(jnp.float32)
            total += jnp.sum(part * part, axis=1, keepdims=True)
        gain = 1.0 / jnp.sqrt(total / jnp.maximum(counts, 1.0) + epsilon)
        for c in range(CHUNKS):
            part = ref[:n, c * width : (c + 1) * width].astype(jnp.float32)
            out[:, c * width : (c + 1) * width] = (part * gain).astype(jnp.bfloat16)

    @pl.when(is_end)
    def _():
        pl.semaphore_signal(barrier, inc=1, device_id={"grp": near}, device_id_type=MESH)
        pl.semaphore_wait(barrier, 1)
        sends = []

        def go(c):
            sends.append(c)
            c.start()

        mask_own(0)
        go(x_copy(z, EX, 0, near))
        go(m_copy(msel, msel_end, 0, near))
        mask_own(1)
        go(x_copy(z, EX, 1, near))
        go(m_copy(mext, mext_end, 1, near))
        for c in range(2, CHUNKS):
            mask_own(c)
            go(x_copy(z, EX, c, near))
        for c in range(CHUNKS):
            part_copy(fe, fe, FE, c, {"grp": near}).wait_recv()
            part_copy(s_all, s_all, SE, c, {"grp": near}).wait_recv()
        for c in sends:
            c.wait_send()
        whiten(w_out, fe, own_counts)

    @pl.when(jnp.logical_not(is_end))
    def _():
        for target in (end, far):
            pl.semaphore_signal(barrier, inc=1, device_id={"grp": target}, device_id_type=MESH)
        for target in flips:
            pl.semaphore_signal(barrier, inc=1, device_id={"seg": target}, device_id_type=MESH)
        pl.semaphore_wait(barrier, 5)
        sends = []

        def go(c):
            sends.append(c)
            c.start()

        def forward(c):
            x_copy(end, EX, c, end).wait_recv()
            go(x_copy(end, XE, c, far))

        def send_own(c):
            mask_own(c)
            go(x_copy(z, XI, c, far))

        send_own(0)
        send_own(1)
        forward(0)
        m_copy(msel_end, msel_end, 0, end).wait_recv()
        msel_sum[...] = msel[...] + msel_end[...]
        go(m_copy(msel_sum, msel_far, 2, far))
        forward(1)
        send_own(2)
        m_copy(mext_end, mext_end, 1, end).wait_recv()
        left[:n] = mext[:n]
        left[n : 2 * n] = mext_end[:n]
        end_counts = counts_column(mext_end[n:], n)
        m_copy(msel_far, msel_far, 2, far).wait_recv()
        left[2 * n : 3 * n] = msel_sum[:n] + msel_far[:n]
        left[3 * n :] = pick[...]
        meta = msel_sum[n:] + msel_far[n:]
        src_counts = counts_column(meta, n)
        sa[n:] = jnp.zeros((META, samples), jnp.bfloat16)
        sa[n:, :n] = meta[:, :n]

        def process(c):
            a, b = c * width, (c + 1) * width
            x_copy(far, XI, c, far).wait_recv()
            x_copy(far_end, XE, c, far).wait_recv()
            coupled = jnp.dot(left[...], xall[:, a:b], preferred_element_type=jnp.float32)
            own_x = xall[pl.ds(z * n, n), a:b].astype(jnp.float32)
            end_x = xall[pl.ds(end * n, n), a:b].astype(jnp.float32)
            fe[:, a:b] = jnp.where(usable(end_counts, c), end_x - coupled[n : 2 * n], 0.0).astype(jnp.bfloat16)
            part = jnp.where(usable(src_counts, c), coupled[3 * n :] - coupled[2 * n : 3 * n], 0.0)
            sa[:n, a:b] = part.astype(jnp.bfloat16)
            go(part_copy(sa, ra, SA, c, {"seg": flips[0]}))
            go(part_copy(fe, fe, FE, c, {"grp": end}))
            fown[:, a:b] = jnp.where(usable(own_counts, c), own_x - coupled[:n], 0.0)

        def stage(mine, arrived, total, kind, c, flip):
            a, b = c * width, (c + 1) * width
            part_copy(mine, arrived, kind, c, {"seg": flip}).wait_recv()
            total[:, a:b] = mine[:, a:b] + arrived[:, a:b]

        for step in range(CHUNKS + 3):
            if step + 2 < CHUNKS:
                forward(step + 2)
            if step + 3 < CHUNKS:
                send_own(step + 3)
            if step < CHUNKS:
                process(step)
            if 0 <= step - 1 < CHUNKS:
                stage(sa, ra, sb, SA, step - 1, flips[0])
                go(part_copy(sb, rb, SB, step - 1, {"seg": flips[1]}))
            if 0 <= step - 2 < CHUNKS:
                stage(sb, rb, sc, SB, step - 2, flips[1])
                go(part_copy(sc, rc, SC, step - 2, {"seg": flips[2]}))
            if 0 <= step - 3 < CHUNKS:
                stage(sc, rc, s_all, SC, step - 3, flips[2])
                go(part_copy(s_all, s_all, SE, step - 3, {"grp": end}))
        whiten(w_out, fown, own_counts)
        for c in sends:
            c.wait_send()

    whiten(s_out, s_all, counts_column(s_all[n:, :n], n))


def gather(strain, counts, working, mixing, owners, offsets):
    n, samples = strain.shape
    wide = mixing.shape[1]
    me = lax.axis_index(("seg", "grp"))
    groups = wide // n
    group = lax.axis_index("seg")
    eff = jnp.where(working > 0, counts, 0)
    meta = jnp.stack([eff // 8, eff % 8]).astype(jnp.bfloat16)
    mext = jnp.concatenate([mixing, jnp.pad(meta, ((0, META - 2), (0, wide - n)))], axis=0)
    rows, metas, picks = [], [], []
    for r in range(ROUNDS):
        here = me == owners[r]
        rows.append(jnp.where(here, lax.dynamic_slice_in_dim(mixing, offsets[r], SRC, 0), 0))
        metas.append(jnp.where(here, lax.dynamic_slice_in_dim(meta, offsets[r], SRC, 1), 0))
        first = jnp.where(owners[r] // groups == group, (owners[r] % groups) * n + offsets[r], -wide)
        column = lax.broadcasted_iota(jnp.int32, (SRC, wide), 1)
        row = lax.broadcasted_iota(jnp.int32, (SRC, wide), 0)
        picks.append(column == row + first)
    sel_meta = jnp.concatenate(metas, axis=1)
    msel = jnp.concatenate(rows + [jnp.pad(sel_meta, ((0, META - 2), (0, wide - n)))], axis=0).astype(jnp.bfloat16)
    pick = jnp.concatenate(picks, axis=0).astype(jnp.bfloat16)
    vmem = pl.BlockSpec(memory_space=pltpu.VMEM)
    part = pltpu.VMEM((n + META, samples), jnp.bfloat16)
    mat = pltpu.VMEM((n + META, wide), jnp.bfloat16)
    return pl.pallas_call(
        gather_kernel,
        out_shape=[jax.ShapeDtypeStruct((n, samples), jnp.bfloat16)] * 2,
        in_specs=[vmem] * 4,
        out_specs=[vmem] * 2,
        scratch_shapes=[
            pltpu.VMEM((wide, samples), jnp.bfloat16),
            pltpu.VMEM((n, samples), jnp.float32),
            pltpu.VMEM((n, samples), jnp.bfloat16),
        ] + [part] * 7 + [mat] * 4 + [
            pltpu.VMEM((4 * n, wide), jnp.bfloat16),
            pltpu.SemaphoreType.DMA((8, CHUNKS)),
            pltpu.SemaphoreType.DMA((8, CHUNKS)),
            pltpu.SemaphoreType.DMA((3,)),
            pltpu.SemaphoreType.DMA((3,)),
        ],
        compiler_params=pltpu.CompilerParams(
            collective_id=0, has_side_effects=True, vmem_limit_bytes=32 * 1024 * 1024),
        name="gather",
    )(strain, mext, msel, pick)


def gather_any(strain, counts, working, mixing, owners, offsets):
    positions = lax.broadcasted_iota(jnp.int32, strain.shape, 1)
    usable = (positions < counts[:, None]) & (working[:, None] > 0)
    masked = jnp.where(usable, strain, jnp.zeros_like(strain))
    coupled = jnp.dot(
        mixing,
        lax.all_gather(masked, "grp", axis=0, tiled=True),
        preferred_element_type=jnp.float32,
    )
    filtered = jnp.where(usable, masked.astype(jnp.float32) - coupled, jnp.float32(0.0))
    sumsq = jnp.sum(filtered * filtered, axis=1)
    spread = jnp.sqrt(sumsq / counts.astype(jnp.float32) + epsilon)
    whitened = (filtered / spread[:, None]).astype(jnp.bfloat16)
    me = lax.axis_index(("seg", "grp"))
    mine = [
        jnp.where(me == owners[r], lax.dynamic_slice_in_dim(whitened, offsets[r], SRC, 0), 0)
        for r in range(ROUNDS)
    ]
    sources = lax.psum(jnp.concatenate(mine, axis=0).astype(jnp.bfloat16), ("seg", "grp"))
    return whitened, sources


def on_device(strain, counts, working, mixing, owners, offsets):
    fits = lax.axis_size("seg") == 8 and lax.axis_size("grp") == 4
    whitened, sources = (gather if fits else gather_any)(strain, counts, working, mixing, owners, offsets)
    return correlate(whitened, sources)


def solution(mesh):
    in_specs = (
        P(("seg", "grp"), None),
        P(("seg", "grp")),
        P(("seg", "grp")),
        P("grp", None),
        P(),
        P(),
    )
    out_specs = P(None, None, None, ("seg", "grp"))
    return jax.shard_map(
        on_device, mesh=mesh, in_specs=in_specs, out_specs=out_specs, check_vma=False
    )
```

```python
import jax
import jax.numpy as jnp
from jax import lax
from jax.experimental import pallas as pl
from jax.experimental.pallas import tpu as pltpu
from jax.sharding import PartitionSpec as P

SRC = 64
LAG = 100
ROUNDS = 2
LAGS = 201
STEP = 10
GROUPS = LAG // STEP
PAD = 128

epsilon = 1e-05
NT = (((1,), (1,)), ((), ()))


def correlate_kernel(w_ref, s_ref, out_hbm, out_ref, wpad, spad, left, right, sem):
    channels, samples = w_ref.shape
    rows = s_ref.shape[0]
    scale = 1.0 / float(samples) ** 0.5
    for pad, ref in ((wpad, w_ref), (spad, s_ref)):
        edge = jnp.zeros((ref.shape[0], PAD), ref.dtype)
        pad[:, :PAD] = edge
        pad[:, PAD + samples :] = edge
        pad[:, PAD : PAD + samples] = ref[...]
    for sign_index, sign in enumerate((1, -1)):
        for group in range(GROUPS):
            start = PAD + sign * STEP * group
            left[sign_index, group * rows : (group + 1) * rows, :] = spad[:, start : start + samples]
        for delta in range(STEP):
            start = PAD - sign * (delta + 1)
            right[sign_index * STEP + delta] = wpad[:, start : start + samples]

    centre = lax.dot_general(s_ref[...], w_ref[...], NT, preferred_element_type=jnp.float32)
    centre = (centre * scale).astype(jnp.bfloat16)
    for r in range(ROUNDS):
        out_ref[r, LAG] = centre[r * SRC : (r + 1) * SRC]
        pltpu.make_async_copy(out_ref.at[r, LAG], out_hbm.at[r, LAG], sem).start()

    def tile(n, carry):
        sign_index = n // (STEP // 2)
        sign = 1 - 2 * sign_index
        first = (n % (STEP // 2)) * 2
        pair = right[pl.ds(n * 2, 2)].reshape(2 * channels, samples)
        products = lax.dot_general(left[sign_index], pair, NT, preferred_element_type=jnp.float32)
        products = (products * scale).astype(jnp.bfloat16)
        for group in range(GROUPS):
            for r in range(ROUNDS):
                row = group * rows + r * SRC
                for d in range(2):
                    lag = LAG + sign * (STEP * group + first + d + 1)
                    out_ref[r, lag] = products[row : row + SRC, d * channels : (d + 1) * channels]
                low = LAG + sign * (STEP * group + first) + 1 - 3 * sign_index
                slab = (r, pl.ds(low, 2))
                pltpu.make_async_copy(out_ref.at[slab], out_hbm.at[slab], sem).start()
        return carry

    lax.fori_loop(0, STEP, tile, 0)
    pltpu.make_async_copy(out_ref, out_hbm, sem).wait()


def correlate(whitened, sources):
    channels, samples = whitened.shape
    rows = sources.shape[0]
    return pl.pallas_call(
        correlate_kernel,
        out_shape=jax.ShapeDtypeStruct((ROUNDS, LAGS, SRC, channels), jnp.bfloat16),
        in_specs=[pl.BlockSpec(memory_space=pltpu.VMEM)] * 2,
        out_specs=pl.BlockSpec(memory_space=pl.ANY),
        scratch_shapes=[
            pltpu.VMEM((ROUNDS, LAGS, SRC, channels), jnp.bfloat16),
            pltpu.VMEM((channels, samples + 2 * PAD), jnp.bfloat16),
            pltpu.VMEM((rows, samples + 2 * PAD), jnp.bfloat16),
            pltpu.VMEM((2, GROUPS * rows, samples), jnp.bfloat16),
            pltpu.VMEM((2 * STEP, channels, samples), jnp.bfloat16),
            pltpu.SemaphoreType.DMA,
        ],
        compiler_params=pltpu.CompilerParams(vmem_limit_bytes=52 * 1024 * 1024),
        cost_estimate=pl.CostEstimate(
            flops=2 * LAGS * rows * channels * samples, bytes_accessed=8 << 20, transcendentals=0
        ),
        name="correlate",
    )(whitened, sources)


EDGES = (0, 2, 4, 6, 8, 10, 12, 13, 14)
CHUNKS = len(EDGES) - 1
META = 16
XI, XE, EX, FE, SA, SB, SC, SE = range(8)
MESH = pl.DeviceIdType.MESH


def counts_column(meta, n):
    lanes = meta[0:1, :n].astype(jnp.float32) * 8.0 + meta[1:2, :n].astype(jnp.float32)
    row = lax.broadcasted_iota(jnp.int32, (n, n), 0)
    lane = lax.broadcasted_iota(jnp.int32, (n, n), 1)
    return jnp.sum(jnp.where(row == lane, lanes, 0.0), axis=1, keepdims=True)


def gather_kernel(owners, offsets, strain, counts, working, mixing, w_out, s_out, mext, msel, xall, fown, fe, sa, ra, sb, rb, sc, rc,
                  s_all, mext_end, msel_end, msel_sum, msel_far, left, send, recv, msend, mrecv):
    n, samples = strain.shape
    wide = mixing.shape[1]
    unit = samples // EDGES[-1]
    edges = [unit * e for e in EDGES]
    seg = lax.axis_index("seg")
    z = lax.axis_index("grp")
    is_end = (z % 3) == 0
    near = 1 + z // 3
    end = 3 * (z - 1)
    far = 3 - z
    far_end = 3 - end
    flips = [seg + 1 - 2 * (seg % 2), seg + 2 - 4 * ((seg // 2) % 2), seg + 4 - 8 * (seg // 4)]

    def cols(c):
        return pl.ds(edges[c], edges[c + 1] - edges[c])

    def copy(src, dst, kind, c, device):
        return pltpu.make_async_remote_copy(
            src_ref=src, dst_ref=dst, send_sem=send.at[kind, c], recv_sem=recv.at[kind, c],
            device_id=device, device_id_type=MESH)

    def block(index, c):
        return xall.at[pl.ds(index * n, n), cols(c)]

    def x_copy(index, kind, c, target):
        return copy(block(index, c), block(index, c), kind, c, {"grp": target})

    def part_copy(src, dst, kind, c, device):
        return copy(src.at[:, cols(c)], dst.at[:, cols(c)], kind, c, device)

    def m_copy(src, dst, index, target):
        return pltpu.make_async_remote_copy(
            src_ref=src, dst_ref=dst, send_sem=msend.at[index], recv_sem=mrecv.at[index],
            device_id={"grp": target}, device_id_type=MESH)

    barrier = pltpu.get_barrier_semaphore()
    live = jnp.where(working[...] > 0, counts[...], 0)
    high = live // 8
    row = lax.broadcasted_iota(jnp.int32, (META, n), 0)
    meta = jnp.where(row == 0, high, jnp.where(row == 1, live - 8 * high, 0)).astype(jnp.float32).astype(jnp.bfloat16)
    mext[:n] = mixing[...]
    mext[n:] = jnp.zeros((META, wide), jnp.bfloat16)
    mext[n:, :n] = meta
    own_counts = counts_column(meta, n)
    me = seg * (wide // n) + z
    chosen, picked = [], []
    for r in range(ROUNDS):
        row = lax.broadcasted_iota(jnp.int32, (SRC, wide), 0)
        column = lax.broadcasted_iota(jnp.int32, (SRC, wide), 1)
        place = (owners[r] - seg * (wide // n)) * n + offsets[r]
        picked.append(jnp.where(column == row + place, 1.0, 0.0))
        place = (owners[r] - me) * (2 * wide) + offsets[r]
        chosen.append(jnp.where(column[:, :n] == row[:, :n] + place, 1.0, 0.0))
    pick = jnp.concatenate(picked, axis=0).astype(jnp.bfloat16)
    chosen = jnp.concatenate(chosen, axis=0).astype(jnp.bfloat16)
    msel[:n] = jnp.dot(chosen, mixing[...], preferred_element_type=jnp.float32).astype(jnp.bfloat16)
    msel[n:] = jnp.zeros((META, wide), jnp.bfloat16)
    msel[n:, :n] = lax.dot_general(meta, chosen, NT, preferred_element_type=jnp.float32).astype(jnp.bfloat16)

    def usable(counts, c):
        position = lax.broadcasted_iota(jnp.int32, (n, edges[c + 1] - edges[c]), 1) + edges[c]
        return position.astype(jnp.float32) < counts

    def mask_own(c):
        part = jnp.where(usable(own_counts, c), strain[:, edges[c] : edges[c + 1]].astype(jnp.float32), 0.0)
        xall[pl.ds(z * n, n), edges[c] : edges[c + 1]] = part.astype(jnp.bfloat16)

    def energy(ref, c):
        part = ref[:n, edges[c] : edges[c + 1]].astype(jnp.float32)
        return jnp.sum(part * part, axis=1, keepdims=True)

    def whiten(out, ref, counts, total):
        gain = 1.0 / jnp.sqrt(total / jnp.maximum(counts, 1.0) + epsilon)
        for c in range(CHUNKS):
            part = ref[:n, edges[c] : edges[c + 1]].astype(jnp.float32)
            out[:, edges[c] : edges[c + 1]] = (part * gain).astype(jnp.bfloat16)

    @pl.when(is_end)
    def _():
        pl.semaphore_signal(barrier, inc=1, device_id={"grp": near}, device_id_type=MESH)
        pl.semaphore_wait(barrier, 1)
        sends = []

        def go(c):
            sends.append(c)
            c.start()

        mask_own(0)
        go(x_copy(z, EX, 0, near))
        go(m_copy(msel, msel_end, 0, near))
        mask_own(1)
        go(x_copy(z, EX, 1, near))
        go(m_copy(mext, mext_end, 1, near))
        for c in range(2, CHUNKS):
            mask_own(c)
            go(x_copy(z, EX, c, near))
        w_total = s_total = jnp.zeros((n, 1), jnp.float32)
        for step in range(CHUNKS + 2):
            if step < CHUNKS:
                part_copy(fe, fe, FE, step, {"grp": near}).wait_recv()
                w_total += energy(fe, step)
            if step == CHUNKS - 1:
                whiten(w_out, fe, own_counts, w_total)
            if step >= 2:
                part_copy(s_all, s_all, SE, step - 2, {"grp": near}).wait_recv()
                s_total += energy(s_all, step - 2)
        whiten(s_out, s_all, counts_column(s_all[n:, :n], n), s_total)
        for c in sends:
            c.wait_send()

    @pl.when(jnp.logical_not(is_end))
    def _():
        for target in (end, far):
            pl.semaphore_signal(barrier, inc=1, device_id={"grp": target}, device_id_type=MESH)
        for target in flips:
            pl.semaphore_signal(barrier, inc=1, device_id={"seg": target}, device_id_type=MESH)
        pl.semaphore_wait(barrier, 5)
        sends = []

        def go(c):
            sends.append(c)
            c.start()

        def forward(c):
            x_copy(end, EX, c, end).wait_recv()
            go(x_copy(end, XE, c, far))

        def send_own(c):
            mask_own(c)
            go(x_copy(z, XI, c, far))

        send_own(0)
        send_own(1)
        forward(0)
        m_copy(msel_end, msel_end, 0, end).wait_recv()
        msel_sum[...] = msel[...] + msel_end[...]
        go(m_copy(msel_sum, msel_far, 2, far))
        forward(1)
        send_own(2)
        m_copy(mext_end, mext_end, 1, end).wait_recv()
        left[:n] = mext[:n]
        left[n : 2 * n] = mext_end[:n]
        end_counts = counts_column(mext_end[n:], n)
        m_copy(msel_far, msel_far, 2, far).wait_recv()
        left[2 * n : 3 * n] = msel_sum[:n] + msel_far[:n]
        left[3 * n :] = pick
        meta = msel_sum[n:] + msel_far[n:]
        src_counts = counts_column(meta, n)
        sa[n:] = jnp.zeros((META, samples), jnp.bfloat16)
        sa[n:, :n] = meta[:, :n]

        def process(c):
            a, b = edges[c], edges[c + 1]
            x_copy(far, XI, c, far).wait_recv()
            x_copy(far_end, XE, c, far).wait_recv()
            coupled = jnp.dot(left[...], xall[:, a:b], preferred_element_type=jnp.float32)
            own_x = xall[pl.ds(z * n, n), a:b].astype(jnp.float32)
            end_x = xall[pl.ds(end * n, n), a:b].astype(jnp.float32)
            fe[:, a:b] = jnp.where(usable(end_counts, c), end_x - coupled[n : 2 * n], 0.0).astype(jnp.bfloat16)
            part = jnp.where(usable(src_counts, c), coupled[3 * n :] - coupled[2 * n : 3 * n], 0.0)
            sa[:n, a:b] = part.astype(jnp.bfloat16)
            go(part_copy(sa, ra, SA, c, {"seg": flips[0]}))
            go(part_copy(fe, fe, FE, c, {"grp": end}))
            own = jnp.where(usable(own_counts, c), own_x - coupled[:n], 0.0)
            fown[:, a:b] = own
            return jnp.sum(own * own, axis=1, keepdims=True)

        def stage(mine, arrived, total, kind, c, flip):
            a, b = edges[c], edges[c + 1]
            part_copy(mine, arrived, kind, c, {"seg": flip}).wait_recv()
            total[:, a:b] = mine[:, a:b] + arrived[:, a:b]

        w_total = s_total = jnp.zeros((n, 1), jnp.float32)
        for step in range(CHUNKS + 3):
            if step + 2 < CHUNKS:
                forward(step + 2)
            if step + 3 < CHUNKS:
                send_own(step + 3)
            if step < CHUNKS:
                w_total += process(step)
            if 0 <= step - 1 < CHUNKS:
                stage(sa, ra, sb, SA, step - 1, flips[0])
                go(part_copy(sb, rb, SB, step - 1, {"seg": flips[1]}))
            if 0 <= step - 2 < CHUNKS:
                stage(sb, rb, sc, SB, step - 2, flips[1])
                go(part_copy(sc, rc, SC, step - 2, {"seg": flips[2]}))
            if 0 <= step - 3 < CHUNKS:
                stage(sc, rc, s_all, SC, step - 3, flips[2])
                go(part_copy(s_all, s_all, SE, step - 3, {"grp": end}))
                s_total += energy(s_all, step - 3)
            if step == CHUNKS:
                whiten(w_out, fown, own_counts, w_total)
        whiten(s_out, s_all, counts_column(s_all[n:, :n], n), s_total)
        for c in sends:
            c.wait_send()


def gather(strain, counts, working, mixing, owners, offsets):
    n, samples = strain.shape
    wide = mixing.shape[1]
    vmem = pl.BlockSpec(memory_space=pltpu.VMEM)
    part = pltpu.VMEM((n + META, samples), jnp.bfloat16)
    mat = pltpu.VMEM((n + META, wide), jnp.bfloat16)
    return pl.pallas_call(
        gather_kernel,
        out_shape=[jax.ShapeDtypeStruct((n, samples), jnp.bfloat16)] * 2,
        in_specs=[pl.BlockSpec(memory_space=pltpu.SMEM)] * 2 + [vmem] * 4,
        out_specs=[vmem] * 2,
        scratch_shapes=[mat] * 2 + [
            pltpu.VMEM((wide, samples), jnp.bfloat16),
            pltpu.VMEM((n, samples), jnp.float32),
            pltpu.VMEM((n, samples), jnp.bfloat16),
        ] + [part] * 7 + [mat] * 4 + [
            pltpu.VMEM((4 * n, wide), jnp.bfloat16),
            pltpu.SemaphoreType.DMA((8, CHUNKS)),
            pltpu.SemaphoreType.DMA((8, CHUNKS)),
            pltpu.SemaphoreType.DMA((3,)),
            pltpu.SemaphoreType.DMA((3,)),
        ],
        compiler_params=pltpu.CompilerParams(
            collective_id=0, has_side_effects=True, vmem_limit_bytes=32 * 1024 * 1024),
        name="gather",
    )(owners, offsets, strain, counts.reshape(1, n), working.reshape(1, n), mixing)


def gather_any(strain, counts, working, mixing, owners, offsets):
    positions = lax.broadcasted_iota(jnp.int32, strain.shape, 1)
    usable = (positions < counts[:, None]) & (working[:, None] > 0)
    masked = jnp.where(usable, strain, jnp.zeros_like(strain))
    coupled = jnp.dot(
        mixing,
        lax.all_gather(masked, "grp", axis=0, tiled=True),
        preferred_element_type=jnp.float32,
    )
    filtered = jnp.where(usable, masked.astype(jnp.float32) - coupled, jnp.float32(0.0))
    sumsq = jnp.sum(filtered * filtered, axis=1)
    spread = jnp.sqrt(sumsq / counts.astype(jnp.float32) + epsilon)
    whitened = (filtered / spread[:, None]).astype(jnp.bfloat16)
    me = lax.axis_index(("seg", "grp"))
    mine = [
        jnp.where(me == owners[r], lax.dynamic_slice_in_dim(whitened, offsets[r], SRC, 0), 0)
        for r in range(ROUNDS)
    ]
    sources = lax.psum(jnp.concatenate(mine, axis=0).astype(jnp.bfloat16), ("seg", "grp"))
    return whitened, sources


def on_device(strain, counts, working, mixing, owners, offsets):
    fits = lax.axis_size("seg") == 8 and lax.axis_size("grp") == 4
    whitened, sources = (gather if fits else gather_any)(strain, counts, working, mixing, owners, offsets)
    return correlate(whitened, sources)


def solution(mesh):
    in_specs = (
        P(("seg", "grp"), None),
        P(("seg", "grp")),
        P(("seg", "grp")),
        P("grp", None),
        P(),
        P(),
    )
    out_specs = P(None, None, None, ("seg", "grp"))
    return jax.shard_map(
        on_device, mesh=mesh, in_specs=in_specs, out_specs=out_specs, check_vma=False
    )
```

```python
import jax
import jax.numpy as jnp
from jax import lax
from jax.experimental import pallas as pl
from jax.experimental.pallas import tpu as pltpu
from jax.sharding import PartitionSpec as P

SRC = 64
LAG = 100
ROUNDS = 2
LAGS = 201
STEP = 10
GROUPS = LAG // STEP
PAD = 128

epsilon = 1e-05
NT = (((1,), (1,)), ((), ()))


def correlate_kernel(w_ref, s_ref, out_hbm, out_ref, wpad, spad, left, right, sem, in_sem):
    channels, samples = w_ref.shape
    rows = s_ref.shape[0]
    scale = 1.0 / float(samples) ** 0.5
    middle = pl.ds(PAD, samples)
    fetches = [
        pltpu.make_async_copy(ref, pad.at[:, middle], in_sem.at[k])
        for k, (pad, ref) in enumerate(((wpad, w_ref), (spad, s_ref)))
    ]
    for fetch in fetches:
        fetch.start()
    for pad in (wpad, spad):
        edge = jnp.zeros((pad.shape[0], PAD), pad.dtype)
        pad[:, :PAD] = edge
        pad[:, PAD + samples :] = edge
    for fetch in fetches:
        fetch.wait()
    for sign_index, sign in enumerate((1, -1)):
        for group in range(GROUPS):
            start = PAD + sign * STEP * group
            left[sign_index, group * rows : (group + 1) * rows, :] = spad[:, start : start + samples]
        for delta in range(STEP):
            start = PAD - sign * (delta + 1)
            right[sign_index * STEP + delta] = wpad[:, start : start + samples]

    centre = lax.dot_general(spad[:, middle], wpad[:, middle], NT, preferred_element_type=jnp.float32)
    centre = (centre * scale).astype(jnp.bfloat16)
    for r in range(ROUNDS):
        out_ref[r, LAG] = centre[r * SRC : (r + 1) * SRC]
        pltpu.make_async_copy(out_ref.at[r, LAG], out_hbm.at[r, LAG], sem).start()

    half = STEP // 2

    def tiles(n, carry):
        results = []
        for sign_index in range(2):
            pair = right[pl.ds(sign_index * STEP + n * 2, 2)].reshape(2 * channels, samples)
            products = lax.dot_general(left[sign_index], pair, NT, preferred_element_type=jnp.float32)
            results.append((products * scale).astype(jnp.bfloat16))
        for sign_index, products in enumerate(results):
            for group in range(GROUPS):
                for r in range(ROUNDS):
                    row = group * rows + r * SRC
                    for d in range(2):
                        offset = STEP * group + 2 * n + d + 1
                        lag = LAG + offset if sign_index == 0 else LAG - offset
                        out_ref[r, lag] = products[row : row + SRC, d * channels : (d + 1) * channels]
        for sign_index in range(2):
            for group in range(GROUPS):
                for r in range(ROUNDS):
                    offset = STEP * group + 2 * n
                    low = LAG + offset + 1 if sign_index == 0 else LAG - offset - 2
                    slab = (r, pl.ds(low, 2))
                    pltpu.make_async_copy(out_ref.at[slab], out_hbm.at[slab], sem).start()
        return carry

    lax.fori_loop(0, half, tiles, 0)
    pltpu.make_async_copy(out_ref, out_hbm, sem).wait()


def correlate(whitened, sources):
    channels, samples = whitened.shape
    rows = sources.shape[0]
    return pl.pallas_call(
        correlate_kernel,
        out_shape=jax.ShapeDtypeStruct((ROUNDS, LAGS, SRC, channels), jnp.bfloat16),
        in_specs=[pl.BlockSpec(memory_space=pl.ANY)] * 2,
        out_specs=pl.BlockSpec(memory_space=pl.ANY),
        scratch_shapes=[
            pltpu.VMEM((ROUNDS, LAGS, SRC, channels), jnp.bfloat16),
            pltpu.VMEM((channels, samples + 2 * PAD), jnp.bfloat16),
            pltpu.VMEM((rows, samples + 2 * PAD), jnp.bfloat16),
            pltpu.VMEM((2, GROUPS * rows, samples), jnp.bfloat16),
            pltpu.VMEM((2 * STEP, channels, samples), jnp.bfloat16),
            pltpu.SemaphoreType.DMA,
            pltpu.SemaphoreType.DMA((2,)),
        ],
        compiler_params=pltpu.CompilerParams(vmem_limit_bytes=56 * 1024 * 1024),
        cost_estimate=pl.CostEstimate(
            flops=2 * LAGS * rows * channels * samples, bytes_accessed=8 << 20, transcendentals=0
        ),
        name="correlate",
    )(whitened, sources)


EDGES = (0, 2, 4, 6, 8, 10, 12, 13, 14)
CHUNKS = len(EDGES) - 1
META = 16
XI, XE, EX, FE, SA, SB, SC, SE = range(8)
MESH = pl.DeviceIdType.MESH


def counts_column(meta, n):
    lanes = meta[0:1, :n].astype(jnp.float32) * 8.0 + meta[1:2, :n].astype(jnp.float32)
    row = lax.broadcasted_iota(jnp.int32, (n, n), 0)
    lane = lax.broadcasted_iota(jnp.int32, (n, n), 1)
    return jnp.sum(jnp.where(row == lane, lanes, 0.0), axis=1, keepdims=True)


def gather_kernel(owners_hbm, offsets_hbm, strain_hbm, counts_hbm, working_hbm, mixing_hbm, w_out, s_out,
                  owners, offsets, strain, counts, working, mixing, in_sem, mext, msel, xall, fown, fe, sa, ra, sb, rb, sc, rc,
                  s_all, mext_end, msel_end, msel_sum, msel_far, left, send, recv, msend, mrecv):
    n, samples = strain.shape
    wide = mixing.shape[1]
    unit = samples // EDGES[-1]
    edges = [unit * e for e in EDGES]
    seg = lax.axis_index("seg")
    z = lax.axis_index("grp")
    is_end = (z % 3) == 0
    near = 1 + z // 3
    end = 3 * (z - 1)
    far = 3 - z
    far_end = 3 - end
    flips = [seg + 1 - 2 * (seg % 2), seg + 2 - 4 * ((seg // 2) % 2), seg + 4 - 8 * (seg // 4)]

    def cols(c):
        return pl.ds(edges[c], edges[c + 1] - edges[c])

    def copy(src, dst, kind, c, device):
        return pltpu.make_async_remote_copy(
            src_ref=src, dst_ref=dst, send_sem=send.at[kind, c], recv_sem=recv.at[kind, c],
            device_id=device, device_id_type=MESH)

    def block(index, c):
        return xall.at[pl.ds(index * n, n), cols(c)]

    def x_copy(index, kind, c, target):
        return copy(block(index, c), block(index, c), kind, c, {"grp": target})

    def part_copy(src, dst, kind, c, device):
        return copy(src.at[:, cols(c)], dst.at[:, cols(c)], kind, c, device)

    def m_copy(src, dst, index, target):
        return pltpu.make_async_remote_copy(
            src_ref=src, dst_ref=dst, send_sem=msend.at[index], recv_sem=mrecv.at[index],
            device_id={"grp": target}, device_id_type=MESH)

    fetches = [
        pltpu.make_async_copy(a, b, in_sem.at[k])
        for k, (a, b) in enumerate(((owners_hbm, owners), (offsets_hbm, offsets), (counts_hbm, counts),
                                    (working_hbm, working), (mixing_hbm, mixing), (strain_hbm, strain)))
    ]
    for fetch in fetches:
        fetch.start()
    barrier = pltpu.get_barrier_semaphore()

    @pl.when(is_end)
    def _():
        pl.semaphore_signal(barrier, inc=1, device_id={"grp": near}, device_id_type=MESH)

    @pl.when(jnp.logical_not(is_end))
    def _():
        for target in (end, far):
            pl.semaphore_signal(barrier, inc=1, device_id={"grp": target}, device_id_type=MESH)
        for target in flips:
            pl.semaphore_signal(barrier, inc=1, device_id={"seg": target}, device_id_type=MESH)

    for fetch in fetches:
        fetch.wait()
    live = jnp.where(working[...] > 0, counts[...], 0)
    high = live // 8
    row = lax.broadcasted_iota(jnp.int32, (META, n), 0)
    meta = jnp.where(row == 0, high, jnp.where(row == 1, live - 8 * high, 0)).astype(jnp.float32).astype(jnp.bfloat16)
    mext[:n] = mixing[...]
    mext[n:] = jnp.zeros((META, wide), jnp.bfloat16)
    mext[n:, :n] = meta
    own_counts = counts_column(meta, n)
    me = seg * (wide // n) + z
    chosen, picked = [], []
    for r in range(ROUNDS):
        row = lax.broadcasted_iota(jnp.int32, (SRC, wide), 0)
        column = lax.broadcasted_iota(jnp.int32, (SRC, wide), 1)
        place = (owners[r] - seg * (wide // n)) * n + offsets[r]
        picked.append(jnp.where(column == row + place, 1.0, 0.0))
        place = (owners[r] - me) * (2 * wide) + offsets[r]
        chosen.append(jnp.where(column[:, :n] == row[:, :n] + place, 1.0, 0.0))
    pick = jnp.concatenate(picked, axis=0).astype(jnp.bfloat16)
    chosen = jnp.concatenate(chosen, axis=0).astype(jnp.bfloat16)
    msel[:n] = jnp.dot(chosen, mixing[...], preferred_element_type=jnp.float32).astype(jnp.bfloat16)
    msel[n:] = jnp.zeros((META, wide), jnp.bfloat16)
    msel[n:, :n] = lax.dot_general(meta, chosen, NT, preferred_element_type=jnp.float32).astype(jnp.bfloat16)

    def usable(counts, c):
        position = lax.broadcasted_iota(jnp.int32, (n, edges[c + 1] - edges[c]), 1) + edges[c]
        return position.astype(jnp.float32) < counts

    def mask_own(c):
        part = jnp.where(usable(own_counts, c), strain[:, edges[c] : edges[c + 1]].astype(jnp.float32), 0.0)
        xall[pl.ds(z * n, n), edges[c] : edges[c + 1]] = part.astype(jnp.bfloat16)

    def energy(ref, c):
        part = ref[:n, edges[c] : edges[c + 1]].astype(jnp.float32)
        return jnp.sum(part * part, axis=1, keepdims=True)

    def whiten(out, ref, counts, total):
        gain = 1.0 / jnp.sqrt(total / jnp.maximum(counts, 1.0) + epsilon)
        for c in range(CHUNKS):
            part = ref[:n, edges[c] : edges[c + 1]].astype(jnp.float32)
            out[:, edges[c] : edges[c + 1]] = (part * gain).astype(jnp.bfloat16)

    @pl.when(is_end)
    def _():
        pl.semaphore_wait(barrier, 1)
        sends = []

        def go(c):
            sends.append(c)
            c.start()

        mask_own(0)
        go(x_copy(z, EX, 0, near))
        go(m_copy(msel, msel_end, 0, near))
        mask_own(1)
        go(x_copy(z, EX, 1, near))
        go(m_copy(mext, mext_end, 1, near))
        for c in range(2, CHUNKS):
            mask_own(c)
            go(x_copy(z, EX, c, near))
        w_total = s_total = jnp.zeros((n, 1), jnp.float32)
        for step in range(CHUNKS + 2):
            if step < CHUNKS:
                part_copy(fe, fe, FE, step, {"grp": near}).wait_recv()
                w_total += energy(fe, step)
            if step == CHUNKS - 1:
                whiten(w_out, fe, own_counts, w_total)
            if step >= 2:
                part_copy(s_all, s_all, SE, step - 2, {"grp": near}).wait_recv()
                s_total += energy(s_all, step - 2)
        whiten(s_out, s_all, counts_column(s_all[n:, :n], n), s_total)
        for c in sends:
            c.wait_send()

    @pl.when(jnp.logical_not(is_end))
    def _():
        pl.semaphore_wait(barrier, 5)
        sends = []

        def go(c):
            sends.append(c)
            c.start()

        def forward(c):
            x_copy(end, EX, c, end).wait_recv()
            go(x_copy(end, XE, c, far))

        def send_own(c):
            mask_own(c)
            go(x_copy(z, XI, c, far))

        send_own(0)
        send_own(1)
        forward(0)
        m_copy(msel_end, msel_end, 0, end).wait_recv()
        msel_sum[...] = msel[...] + msel_end[...]
        go(m_copy(msel_sum, msel_far, 2, far))
        forward(1)
        send_own(2)
        m_copy(mext_end, mext_end, 1, end).wait_recv()
        left[:n] = mext[:n]
        left[n : 2 * n] = mext_end[:n]
        end_counts = counts_column(mext_end[n:], n)
        m_copy(msel_far, msel_far, 2, far).wait_recv()
        left[2 * n : 3 * n] = msel_sum[:n] + msel_far[:n]
        left[3 * n :] = pick
        meta = msel_sum[n:] + msel_far[n:]
        src_counts = counts_column(meta, n)
        sa[n:] = jnp.zeros((META, samples), jnp.bfloat16)
        sa[n:, :n] = meta[:, :n]

        def process(c):
            a, b = edges[c], edges[c + 1]
            x_copy(far, XI, c, far).wait_recv()
            x_copy(far_end, XE, c, far).wait_recv()
            coupled = jnp.dot(left[...], xall[:, a:b], preferred_element_type=jnp.float32)
            own_x = xall[pl.ds(z * n, n), a:b].astype(jnp.float32)
            end_x = xall[pl.ds(end * n, n), a:b].astype(jnp.float32)
            fe[:, a:b] = jnp.where(usable(end_counts, c), end_x - coupled[n : 2 * n], 0.0).astype(jnp.bfloat16)
            part = jnp.where(usable(src_counts, c), coupled[3 * n :] - coupled[2 * n : 3 * n], 0.0)
            sa[:n, a:b] = part.astype(jnp.bfloat16)
            go(part_copy(sa, ra, SA, c, {"seg": flips[0]}))
            go(part_copy(fe, fe, FE, c, {"grp": end}))
            own = jnp.where(usable(own_counts, c), own_x - coupled[:n], 0.0)
            fown[:, a:b] = own
            return jnp.sum(own * own, axis=1, keepdims=True)

        def stage(mine, arrived, total, kind, c, flip):
            a, b = edges[c], edges[c + 1]
            part_copy(mine, arrived, kind, c, {"seg": flip}).wait_recv()
            total[:, a:b] = mine[:, a:b] + arrived[:, a:b]

        w_total = s_total = jnp.zeros((n, 1), jnp.float32)
        for step in range(CHUNKS + 3):
            if step + 2 < CHUNKS:
                forward(step + 2)
            if step + 3 < CHUNKS:
                send_own(step + 3)
            if step < CHUNKS:
                w_total += process(step)
            if 0 <= step - 1 < CHUNKS:
                stage(sa, ra, sb, SA, step - 1, flips[0])
                go(part_copy(sb, rb, SB, step - 1, {"seg": flips[1]}))
            if 0 <= step - 2 < CHUNKS:
                stage(sb, rb, sc, SB, step - 2, flips[1])
                go(part_copy(sc, rc, SC, step - 2, {"seg": flips[2]}))
            if 0 <= step - 3 < CHUNKS:
                stage(sc, rc, s_all, SC, step - 3, flips[2])
                go(part_copy(s_all, s_all, SE, step - 3, {"grp": end}))
                s_total += energy(s_all, step - 3)
            if step == CHUNKS:
                whiten(w_out, fown, own_counts, w_total)
        whiten(s_out, s_all, counts_column(s_all[n:, :n], n), s_total)
        for c in sends:
            c.wait_send()


def gather(strain, counts, working, mixing, owners, offsets):
    n, samples = strain.shape
    wide = mixing.shape[1]
    vmem = pl.BlockSpec(memory_space=pltpu.VMEM)
    part = pltpu.VMEM((n + META, samples), jnp.bfloat16)
    mat = pltpu.VMEM((n + META, wide), jnp.bfloat16)
    return pl.pallas_call(
        gather_kernel,
        out_shape=[jax.ShapeDtypeStruct((n, samples), jnp.bfloat16)] * 2,
        in_specs=[pl.BlockSpec(memory_space=pl.ANY)] * 6,
        out_specs=[vmem] * 2,
        scratch_shapes=[pltpu.SMEM((ROUNDS,), jnp.int32)] * 2 + [
            pltpu.VMEM((n, samples), jnp.bfloat16),
            pltpu.VMEM((1, n), jnp.int32),
            pltpu.VMEM((1, n), jnp.int32),
            pltpu.VMEM((n, wide), jnp.bfloat16),
            pltpu.SemaphoreType.DMA((6,)),
        ] + [mat] * 2 + [
            pltpu.VMEM((wide, samples), jnp.bfloat16),
            pltpu.VMEM((n, samples), jnp.float32),
            pltpu.VMEM((n, samples), jnp.bfloat16),
        ] + [part] * 7 + [mat] * 4 + [
            pltpu.VMEM((4 * n, wide), jnp.bfloat16),
            pltpu.SemaphoreType.DMA((8, CHUNKS)),
            pltpu.SemaphoreType.DMA((8, CHUNKS)),
            pltpu.SemaphoreType.DMA((3,)),
            pltpu.SemaphoreType.DMA((3,)),
        ],
        compiler_params=pltpu.CompilerParams(
            collective_id=0, has_side_effects=True, vmem_limit_bytes=56 * 1024 * 1024),
        name="gather",
    )(owners, offsets, strain, counts.reshape(1, n), working.reshape(1, n), mixing)


def gather_any(strain, counts, working, mixing, owners, offsets):
    positions = lax.broadcasted_iota(jnp.int32, strain.shape, 1)
    usable = (positions < counts[:, None]) & (working[:, None] > 0)
    masked = jnp.where(usable, strain, jnp.zeros_like(strain))
    coupled = jnp.dot(
        mixing,
        lax.all_gather(masked, "grp", axis=0, tiled=True),
        preferred_element_type=jnp.float32,
    )
    filtered = jnp.where(usable, masked.astype(jnp.float32) - coupled, jnp.float32(0.0))
    sumsq = jnp.sum(filtered * filtered, axis=1)
    spread = jnp.sqrt(sumsq / counts.astype(jnp.float32) + epsilon)
    whitened = (filtered / spread[:, None]).astype(jnp.bfloat16)
    me = lax.axis_index(("seg", "grp"))
    mine = [
        jnp.where(me == owners[r], lax.dynamic_slice_in_dim(whitened, offsets[r], SRC, 0), 0)
        for r in range(ROUNDS)
    ]
    sources = lax.psum(jnp.concatenate(mine, axis=0).astype(jnp.bfloat16), ("seg", "grp"))
    return whitened, sources


def on_device(strain, counts, working, mixing, owners, offsets):
    fits = lax.axis_size("seg") == 8 and lax.axis_size("grp") == 4
    whitened, sources = (gather if fits else gather_any)(strain, counts, working, mixing, owners, offsets)
    return correlate(whitened, sources)


def solution(mesh):
    in_specs = (
        P(("seg", "grp"), None),
        P(("seg", "grp")),
        P(("seg", "grp")),
        P("grp", None),
        P(),
        P(),
    )
    out_specs = P(None, None, None, ("seg", "grp"))
    return jax.shard_map(
        on_device, mesh=mesh, in_specs=in_specs, out_specs=out_specs, check_vma=False
    )
```

```python
import jax
import jax.numpy as jnp
from jax import lax
from jax.experimental import pallas as pl
from jax.experimental.pallas import tpu as pltpu
from jax.sharding import PartitionSpec as P

SRC = 64
LAG = 100
ROUNDS = 2
LAGS = 201
STEP = 4
GROUPS = LAG // STEP
PAD = 128

epsilon = 1e-05
NT = (((1,), (1,)), ((), ()))


def correlate_kernel(w_ref, s_ref, out_hbm, out_ref, wpad, spad, left, right, sem, in_sem):
    channels, samples = w_ref.shape
    rows = s_ref.shape[0]
    scale = 1.0 / float(samples) ** 0.5
    middle = pl.ds(PAD, samples)
    fetches = [
        pltpu.make_async_copy(ref, pad.at[:, middle], in_sem.at[k])
        for k, (pad, ref) in enumerate(((wpad, w_ref), (spad, s_ref)))
    ]
    for fetch in fetches:
        fetch.start()
    for pad in (wpad, spad):
        edge = jnp.zeros((pad.shape[0], PAD), pad.dtype)
        pad[:, :PAD] = edge
        pad[:, PAD + samples :] = edge
    for fetch in fetches:
        fetch.wait()
    for sign_index, sign in enumerate((1, -1)):
        for group in range(GROUPS):
            start = PAD + sign * STEP * group
            left[sign_index, group * rows : (group + 1) * rows, :] = spad[:, start : start + samples]
        for delta in range(STEP):
            start = PAD - sign * (delta + 1)
            right[sign_index * STEP + delta] = wpad[:, start : start + samples]

    centre = lax.dot_general(spad[:, middle], wpad[:, middle], NT, preferred_element_type=jnp.float32)
    centre = (centre * scale).astype(jnp.bfloat16)
    for r in range(ROUNDS):
        out_ref[r, LAG] = centre[r * SRC : (r + 1) * SRC]
        pltpu.make_async_copy(out_ref.at[r, LAG], out_hbm.at[r, LAG], sem).start()

    half = STEP // 2

    def tiles(n, carry):
        for sign_index in range(2):
            pair = right[pl.ds(sign_index * STEP + n * 2, 2)].reshape(2 * channels, samples)
            products = lax.dot_general(left[sign_index], pair, NT, preferred_element_type=jnp.float32)
            products = (products * scale).astype(jnp.bfloat16)
            for group in range(GROUPS):
                for r in range(ROUNDS):
                    row = group * rows + r * SRC
                    for d in range(2):
                        offset = STEP * group + 2 * n + d + 1
                        lag = LAG + offset if sign_index == 0 else LAG - offset
                        out_ref[r, lag] = products[row : row + SRC, d * channels : (d + 1) * channels]
                    offset = STEP * group + 2 * n
                    low = LAG + offset + 1 if sign_index == 0 else LAG - offset - 2
                    slab = (r, pl.ds(low, 2))
                    pltpu.make_async_copy(out_ref.at[slab], out_hbm.at[slab], sem).start()
        return carry

    lax.fori_loop(0, half, tiles, 0)
    pltpu.make_async_copy(out_ref, out_hbm, sem).wait()


def correlate(whitened, sources):
    channels, samples = whitened.shape
    rows = sources.shape[0]
    return pl.pallas_call(
        correlate_kernel,
        out_shape=jax.ShapeDtypeStruct((ROUNDS, LAGS, SRC, channels), jnp.bfloat16),
        in_specs=[pl.BlockSpec(memory_space=pl.ANY)] * 2,
        out_specs=pl.BlockSpec(memory_space=pl.ANY),
        scratch_shapes=[
            pltpu.VMEM((ROUNDS, LAGS, SRC, channels), jnp.bfloat16),
            pltpu.VMEM((channels, samples + 2 * PAD), jnp.bfloat16),
            pltpu.VMEM((rows, samples + 2 * PAD), jnp.bfloat16),
            pltpu.VMEM((2, GROUPS * rows, samples), jnp.bfloat16),
            pltpu.VMEM((2 * STEP, channels, samples), jnp.bfloat16),
            pltpu.SemaphoreType.DMA,
            pltpu.SemaphoreType.DMA((2,)),
        ],
        compiler_params=pltpu.CompilerParams(vmem_limit_bytes=56 * 1024 * 1024),
        cost_estimate=pl.CostEstimate(
            flops=2 * LAGS * rows * channels * samples, bytes_accessed=8 << 20, transcendentals=0
        ),
        name="correlate",
    )(whitened, sources)


EDGES = (0, 2, 4, 6, 8, 10, 12, 13, 14)
CHUNKS = len(EDGES) - 1
META = 16
XI, XE, EX, FE, SA, SB, SC, SE = range(8)
MESH = pl.DeviceIdType.MESH


def counts_column(meta, n):
    lanes = meta[0:1, :n].astype(jnp.float32) * 8.0 + meta[1:2, :n].astype(jnp.float32)
    row = lax.broadcasted_iota(jnp.int32, (n, n), 0)
    lane = lax.broadcasted_iota(jnp.int32, (n, n), 1)
    return jnp.sum(jnp.where(row == lane, lanes, 0.0), axis=1, keepdims=True)


def gather_kernel(owners_hbm, offsets_hbm, strain_hbm, counts_hbm, working_hbm, mixing_hbm, w_out, s_out,
                  owners, offsets, strain, counts, working, mixing, in_sem, mext, msel, xall, fown, fe, sa, ra, sb, rb, sc, rc,
                  s_all, mext_end, msel_end, msel_sum, msel_far, left, send, recv, msend, mrecv):
    n, samples = strain.shape
    wide = mixing.shape[1]
    unit = samples // EDGES[-1]
    edges = [unit * e for e in EDGES]
    seg = lax.axis_index("seg")
    z = lax.axis_index("grp")
    is_end = (z % 3) == 0
    near = 1 + z // 3
    end = 3 * (z - 1)
    far = 3 - z
    far_end = 3 - end
    flips = [seg + 1 - 2 * (seg % 2), seg + 2 - 4 * ((seg // 2) % 2), seg + 4 - 8 * (seg // 4)]

    def cols(c):
        return pl.ds(edges[c], edges[c + 1] - edges[c])

    def copy(src, dst, kind, c, device):
        return pltpu.make_async_remote_copy(
            src_ref=src, dst_ref=dst, send_sem=send.at[kind, c], recv_sem=recv.at[kind, c],
            device_id=device, device_id_type=MESH)

    def block(index, c):
        return xall.at[pl.ds(index * n, n), cols(c)]

    def x_copy(index, kind, c, target):
        return copy(block(index, c), block(index, c), kind, c, {"grp": target})

    def part_copy(src, dst, kind, c, device):
        return copy(src.at[:, cols(c)], dst.at[:, cols(c)], kind, c, device)

    def m_copy(src, dst, index, target):
        return pltpu.make_async_remote_copy(
            src_ref=src, dst_ref=dst, send_sem=msend.at[index], recv_sem=mrecv.at[index],
            device_id={"grp": target}, device_id_type=MESH)

    fetches = [
        pltpu.make_async_copy(a, b, in_sem.at[k])
        for k, (a, b) in enumerate(((owners_hbm, owners), (offsets_hbm, offsets), (counts_hbm, counts),
                                    (working_hbm, working), (mixing_hbm, mixing), (strain_hbm, strain)))
    ]
    for fetch in fetches:
        fetch.start()
    barrier = pltpu.get_barrier_semaphore()

    @pl.when(is_end)
    def _():
        pl.semaphore_signal(barrier, inc=1, device_id={"grp": near}, device_id_type=MESH)

    @pl.when(jnp.logical_not(is_end))
    def _():
        for target in (end, far):
            pl.semaphore_signal(barrier, inc=1, device_id={"grp": target}, device_id_type=MESH)
        for target in flips:
            pl.semaphore_signal(barrier, inc=1, device_id={"seg": target}, device_id_type=MESH)

    for fetch in fetches:
        fetch.wait()
    live = jnp.where(working[...] > 0, counts[...], 0)
    high = live // 8
    row = lax.broadcasted_iota(jnp.int32, (META, n), 0)
    meta = jnp.where(row == 0, high, jnp.where(row == 1, live - 8 * high, 0)).astype(jnp.float32).astype(jnp.bfloat16)
    mext[:n] = mixing[...]
    mext[n:] = jnp.zeros((META, wide), jnp.bfloat16)
    mext[n:, :n] = meta
    own_counts = counts_column(meta, n)
    me = seg * (wide // n) + z
    chosen, picked = [], []
    for r in range(ROUNDS):
        row = lax.broadcasted_iota(jnp.int32, (SRC, wide), 0)
        column = lax.broadcasted_iota(jnp.int32, (SRC, wide), 1)
        place = (owners[r] - seg * (wide // n)) * n + offsets[r]
        picked.append(jnp.where(column == row + place, 1.0, 0.0))
        place = (owners[r] - me) * (2 * wide) + offsets[r]
        chosen.append(jnp.where(column[:, :n] == row[:, :n] + place, 1.0, 0.0))
    pick = jnp.concatenate(picked, axis=0).astype(jnp.bfloat16)
    chosen = jnp.concatenate(chosen, axis=0).astype(jnp.bfloat16)
    msel[:n] = jnp.dot(chosen, mixing[...], preferred_element_type=jnp.float32).astype(jnp.bfloat16)
    msel[n:] = jnp.zeros((META, wide), jnp.bfloat16)
    msel[n:, :n] = lax.dot_general(meta, chosen, NT, preferred_element_type=jnp.float32).astype(jnp.bfloat16)

    def usable(counts, c):
        position = lax.broadcasted_iota(jnp.int32, (n, edges[c + 1] - edges[c]), 1) + edges[c]
        return position.astype(jnp.float32) < counts

    def mask_own(c):
        part = jnp.where(usable(own_counts, c), strain[:, edges[c] : edges[c + 1]].astype(jnp.float32), 0.0)
        xall[pl.ds(z * n, n), edges[c] : edges[c + 1]] = part.astype(jnp.bfloat16)

    def energy(ref, c):
        part = ref[:n, edges[c] : edges[c + 1]].astype(jnp.float32)
        return jnp.sum(part * part, axis=1, keepdims=True)

    def whiten(out, ref, counts, total):
        gain = 1.0 / jnp.sqrt(total / jnp.maximum(counts, 1.0) + epsilon)
        for c in range(CHUNKS):
            part = ref[:n, edges[c] : edges[c + 1]].astype(jnp.float32)
            out[:, edges[c] : edges[c + 1]] = (part * gain).astype(jnp.bfloat16)

    @pl.when(is_end)
    def _():
        pl.semaphore_wait(barrier, 1)
        sends = []

        def go(c):
            sends.append(c)
            c.start()

        mask_own(0)
        go(x_copy(z, EX, 0, near))
        go(m_copy(msel, msel_end, 0, near))
        mask_own(1)
        go(x_copy(z, EX, 1, near))
        go(m_copy(mext, mext_end, 1, near))
        for c in range(2, CHUNKS):
            mask_own(c)
            go(x_copy(z, EX, c, near))
        w_total = s_total = jnp.zeros((n, 1), jnp.float32)
        for step in range(CHUNKS + 2):
            if step < CHUNKS:
                part_copy(fe, fe, FE, step, {"grp": near}).wait_recv()
                w_total += energy(fe, step)
            if step == CHUNKS - 1:
                whiten(w_out, fe, own_counts, w_total)
            if step >= 2:
                part_copy(s_all, s_all, SE, step - 2, {"grp": near}).wait_recv()
                s_total += energy(s_all, step - 2)
        whiten(s_out, s_all, counts_column(s_all[n:, :n], n), s_total)
        for c in sends:
            c.wait_send()

    @pl.when(jnp.logical_not(is_end))
    def _():
        pl.semaphore_wait(barrier, 5)
        sends = []

        def go(c):
            sends.append(c)
            c.start()

        def forward(c):
            x_copy(end, EX, c, end).wait_recv()
            go(x_copy(end, XE, c, far))

        def send_own(c):
            mask_own(c)
            go(x_copy(z, XI, c, far))

        send_own(0)
        send_own(1)
        forward(0)
        m_copy(msel_end, msel_end, 0, end).wait_recv()
        msel_sum[...] = msel[...] + msel_end[...]
        go(m_copy(msel_sum, msel_far, 2, far))
        forward(1)
        send_own(2)
        forward(2)
        send_own(3)
        m_copy(mext_end, mext_end, 1, end).wait_recv()
        left[:n] = mext[:n]
        left[n : 2 * n] = mext_end[:n]
        end_counts = counts_column(mext_end[n:], n)
        m_copy(msel_far, msel_far, 2, far).wait_recv()
        left[2 * n : 3 * n] = msel_sum[:n] + msel_far[:n]
        left[3 * n :] = pick
        meta = msel_sum[n:] + msel_far[n:]
        src_counts = counts_column(meta, n)
        sa[n:] = jnp.zeros((META, samples), jnp.bfloat16)
        sa[n:, :n] = meta[:, :n]

        def process(c):
            a, b = edges[c], edges[c + 1]
            x_copy(far, XI, c, far).wait_recv()
            x_copy(far_end, XE, c, far).wait_recv()
            coupled = jnp.dot(left[...], xall[:, a:b], preferred_element_type=jnp.float32)
            own_x = xall[pl.ds(z * n, n), a:b].astype(jnp.float32)
            end_x = xall[pl.ds(end * n, n), a:b].astype(jnp.float32)
            fe[:, a:b] = jnp.where(usable(end_counts, c), end_x - coupled[n : 2 * n], 0.0).astype(jnp.bfloat16)
            part = jnp.where(usable(src_counts, c), coupled[3 * n :] - coupled[2 * n : 3 * n], 0.0)
            sa[:n, a:b] = part.astype(jnp.bfloat16)
            go(part_copy(sa, ra, SA, c, {"seg": flips[0]}))
            go(part_copy(fe, fe, FE, c, {"grp": end}))
            own = jnp.where(usable(own_counts, c), own_x - coupled[:n], 0.0)
            fown[:, a:b] = own
            return jnp.sum(own * own, axis=1, keepdims=True)

        def stage(mine, arrived, total, kind, c, flip):
            a, b = edges[c], edges[c + 1]
            part_copy(mine, arrived, kind, c, {"seg": flip}).wait_recv()
            total[:, a:b] = mine[:, a:b] + arrived[:, a:b]

        w_total = s_total = jnp.zeros((n, 1), jnp.float32)
        for step in range(CHUNKS + 3):
            if step + 3 < CHUNKS:
                forward(step + 3)
            if step + 4 < CHUNKS:
                send_own(step + 4)
            if step < CHUNKS:
                w_total += process(step)
            if 0 <= step - 1 < CHUNKS:
                stage(sa, ra, sb, SA, step - 1, flips[0])
                go(part_copy(sb, rb, SB, step - 1, {"seg": flips[1]}))
            if 0 <= step - 2 < CHUNKS:
                stage(sb, rb, sc, SB, step - 2, flips[1])
                go(part_copy(sc, rc, SC, step - 2, {"seg": flips[2]}))
            if 0 <= step - 3 < CHUNKS:
                stage(sc, rc, s_all, SC, step - 3, flips[2])
                go(part_copy(s_all, s_all, SE, step - 3, {"grp": end}))
                s_total += energy(s_all, step - 3)
            if step == CHUNKS:
                whiten(w_out, fown, own_counts, w_total)
        whiten(s_out, s_all, counts_column(s_all[n:, :n], n), s_total)
        for c in sends:
            c.wait_send()


def gather(strain, counts, working, mixing, owners, offsets):
    n, samples = strain.shape
    wide = mixing.shape[1]
    vmem = pl.BlockSpec(memory_space=pltpu.VMEM)
    part = pltpu.VMEM((n + META, samples), jnp.bfloat16)
    mat = pltpu.VMEM((n + META, wide), jnp.bfloat16)
    return pl.pallas_call(
        gather_kernel,
        out_shape=[jax.ShapeDtypeStruct((n, samples), jnp.bfloat16)] * 2,
        in_specs=[pl.BlockSpec(memory_space=pl.ANY)] * 6,
        out_specs=[vmem] * 2,
        scratch_shapes=[pltpu.SMEM((ROUNDS,), jnp.int32)] * 2 + [
            pltpu.VMEM((n, samples), jnp.bfloat16),
            pltpu.VMEM((1, n), jnp.int32),
            pltpu.VMEM((1, n), jnp.int32),
            pltpu.VMEM((n, wide), jnp.bfloat16),
            pltpu.SemaphoreType.DMA((6,)),
        ] + [mat] * 2 + [
            pltpu.VMEM((wide, samples), jnp.bfloat16),
            pltpu.VMEM((n, samples), jnp.float32),
            pltpu.VMEM((n, samples), jnp.bfloat16),
        ] + [part] * 7 + [mat] * 4 + [
            pltpu.VMEM((4 * n, wide), jnp.bfloat16),
            pltpu.SemaphoreType.DMA((8, CHUNKS)),
            pltpu.SemaphoreType.DMA((8, CHUNKS)),
            pltpu.SemaphoreType.DMA((3,)),
            pltpu.SemaphoreType.DMA((3,)),
        ],
        compiler_params=pltpu.CompilerParams(
            collective_id=0, has_side_effects=True, vmem_limit_bytes=56 * 1024 * 1024),
        name="gather",
    )(owners, offsets, strain, counts.reshape(1, n), working.reshape(1, n), mixing)


def gather_any(strain, counts, working, mixing, owners, offsets):
    positions = lax.broadcasted_iota(jnp.int32, strain.shape, 1)
    usable = (positions < counts[:, None]) & (working[:, None] > 0)
    masked = jnp.where(usable, strain, jnp.zeros_like(strain))
    coupled = jnp.dot(
        mixing,
        lax.all_gather(masked, "grp", axis=0, tiled=True),
        preferred_element_type=jnp.float32,
    )
    filtered = jnp.where(usable, masked.astype(jnp.float32) - coupled, jnp.float32(0.0))
    sumsq = jnp.sum(filtered * filtered, axis=1)
    spread = jnp.sqrt(sumsq / counts.astype(jnp.float32) + epsilon)
    whitened = (filtered / spread[:, None]).astype(jnp.bfloat16)
    me = lax.axis_index(("seg", "grp"))
    mine = [
        jnp.where(me == owners[r], lax.dynamic_slice_in_dim(whitened, offsets[r], SRC, 0), 0)
        for r in range(ROUNDS)
    ]
    sources = lax.psum(jnp.concatenate(mine, axis=0).astype(jnp.bfloat16), ("seg", "grp"))
    return whitened, sources


def on_device(strain, counts, working, mixing, owners, offsets):
    fits = lax.axis_size("seg") == 8 and lax.axis_size("grp") == 4
    whitened, sources = (gather if fits else gather_any)(strain, counts, working, mixing, owners, offsets)
    return correlate(whitened, sources)


def solution(mesh):
    in_specs = (
        P(("seg", "grp"), None),
        P(("seg", "grp")),
        P(("seg", "grp")),
        P("grp", None),
        P(),
        P(),
    )
    out_specs = P(None, None, None, ("seg", "grp"))
    return jax.shard_map(
        on_device, mesh=mesh, in_specs=in_specs, out_specs=out_specs, check_vma=False
    )
```

```python
import jax
import jax.numpy as jnp
from jax import lax
from jax.experimental import pallas as pl
from jax.experimental.pallas import tpu as pltpu
from jax.sharding import PartitionSpec as P

SRC = 64
LAG = 100
ROUNDS = 2
LAGS = 201
STEP = 10
GROUPS = LAG // STEP
PAD = 128

epsilon = 1e-05
NT = (((1,), (1,)), ((), ()))


def correlate_kernel(w_ref, s_ref, out_hbm, out_ref, wpad, spad, left, right, sem, in_sem):
    channels, samples = w_ref.shape
    rows = s_ref.shape[0]
    scale = 1.0 / float(samples) ** 0.5
    middle = pl.ds(PAD, samples)
    fetches = [
        pltpu.make_async_copy(ref, pad.at[:, middle], in_sem.at[k])
        for k, (pad, ref) in enumerate(((wpad, w_ref), (spad, s_ref)))
    ]
    for fetch in fetches:
        fetch.start()
    for pad in (wpad, spad):
        edge = jnp.zeros((pad.shape[0], PAD), pad.dtype)
        pad[:, :PAD] = edge
        pad[:, PAD + samples :] = edge
    for fetch in fetches:
        fetch.wait()
    half = STEP // 2

    def shift_sources(sign_index, group):
        start = PAD + (1 - 2 * sign_index) * STEP * group
        left[sign_index, group * rows : (group + 1) * rows, :] = spad[:, start : start + samples]

    def shift_pair(tile):
        for delta in (2 * (tile % half), 2 * (tile % half) + 1):
            start = PAD - (1 - 2 * (tile // half)) * (delta + 1)
            right[tile // half * STEP + delta] = wpad[:, start : start + samples]

    shift_pair(0)
    for group in range(GROUPS):
        shift_sources(0, group)

    centre = lax.dot_general(spad[:, middle], wpad[:, middle], NT, preferred_element_type=jnp.float32)
    centre = (centre * scale).astype(jnp.bfloat16)
    for r in range(ROUNDS):
        out_ref[r, LAG] = centre[r * SRC : (r + 1) * SRC]
        pltpu.make_async_copy(out_ref.at[r, LAG], out_hbm.at[r, LAG], sem).start()

    for tile in range(2 * half):
        sign_index, n = tile // half, tile % half
        if tile + 1 < 2 * half:
            shift_pair(tile + 1)
        if sign_index == 0:
            shift_sources(1, 2 * n)
            shift_sources(1, 2 * n + 1)
        pair = right[2 * tile : 2 * tile + 2].reshape(2 * channels, samples)
        products = lax.dot_general(left[sign_index], pair, NT, preferred_element_type=jnp.float32)
        products = (products * scale).astype(jnp.bfloat16)
        slabs = []
        for group in range(GROUPS):
            for r in range(ROUNDS):
                row = group * rows + r * SRC
                offset = STEP * group + 2 * n
                for d in range(2):
                    lag = LAG + (1 - 2 * sign_index) * (offset + d + 1)
                    out_ref[r, lag] = products[row : row + SRC, d * channels : (d + 1) * channels]
                slabs.append((r, pl.ds(LAG + offset + 1 if sign_index == 0 else LAG - offset - 2, 2)))
        for slab in slabs:
            pltpu.make_async_copy(out_ref.at[slab], out_hbm.at[slab], sem).start()
    pltpu.make_async_copy(out_ref, out_hbm, sem).wait()


def correlate(whitened, sources):
    channels, samples = whitened.shape
    rows = sources.shape[0]
    return pl.pallas_call(
        correlate_kernel,
        out_shape=jax.ShapeDtypeStruct((ROUNDS, LAGS, SRC, channels), jnp.bfloat16),
        in_specs=[pl.BlockSpec(memory_space=pl.ANY)] * 2,
        out_specs=pl.BlockSpec(memory_space=pl.ANY),
        scratch_shapes=[
            pltpu.VMEM((ROUNDS, LAGS, SRC, channels), jnp.bfloat16),
            pltpu.VMEM((channels, samples + 2 * PAD), jnp.bfloat16),
            pltpu.VMEM((rows, samples + 2 * PAD), jnp.bfloat16),
            pltpu.VMEM((2, GROUPS * rows, samples), jnp.bfloat16),
            pltpu.VMEM((2 * STEP, channels, samples), jnp.bfloat16),
            pltpu.SemaphoreType.DMA,
            pltpu.SemaphoreType.DMA((2,)),
        ],
        compiler_params=pltpu.CompilerParams(vmem_limit_bytes=56 * 1024 * 1024),
        cost_estimate=pl.CostEstimate(
            flops=2 * LAGS * rows * channels * samples, bytes_accessed=8 << 20, transcendentals=0
        ),
        name="correlate",
    )(whitened, sources)


EDGES = (0, 2, 4, 6, 8, 10, 12, 13, 14)
CHUNKS = len(EDGES) - 1
META = 16
XI, XE, EX, FE, SA, SB, SC, SE = range(8)
MESH = pl.DeviceIdType.MESH


def counts_column(meta, n):
    lanes = meta[0:1, :n].astype(jnp.float32) * 8.0 + meta[1:2, :n].astype(jnp.float32)
    row = lax.broadcasted_iota(jnp.int32, (n, n), 0)
    lane = lax.broadcasted_iota(jnp.int32, (n, n), 1)
    return jnp.sum(jnp.where(row == lane, lanes, 0.0), axis=1, keepdims=True)


def gather_kernel(owners_hbm, offsets_hbm, strain_hbm, counts_hbm, working_hbm, mixing_hbm, w_out, s_out,
                  owners, offsets, strain, counts, working, mixing, in_sem, mext, msel, xall, fown, fe, sa, ra, sb, rb, sc, rc,
                  s_all, mext_end, msel_end, msel_sum, msel_far, left, send, recv, msend, mrecv):
    n, samples = strain.shape
    wide = mixing.shape[1]
    unit = samples // EDGES[-1]
    edges = [unit * e for e in EDGES]
    seg = lax.axis_index("seg")
    z = lax.axis_index("grp")
    is_end = (z % 3) == 0
    near = 1 + z // 3
    end = 3 * (z - 1)
    far = 3 - z
    far_end = 3 - end
    flips = [seg + 1 - 2 * (seg % 2), seg + 2 - 4 * ((seg // 2) % 2), seg + 4 - 8 * (seg // 4)]

    def cols(c):
        return pl.ds(edges[c], edges[c + 1] - edges[c])

    def copy(src, dst, kind, c, device):
        return pltpu.make_async_remote_copy(
            src_ref=src, dst_ref=dst, send_sem=send.at[kind, c], recv_sem=recv.at[kind, c],
            device_id=device, device_id_type=MESH)

    def block(index, c):
        return xall.at[pl.ds(index * n, n), cols(c)]

    def x_copy(index, kind, c, target):
        return copy(block(index, c), block(index, c), kind, c, {"grp": target})

    def part_copy(src, dst, kind, c, device):
        return copy(src.at[:, cols(c)], dst.at[:, cols(c)], kind, c, device)

    def m_copy(src, dst, index, target):
        return pltpu.make_async_remote_copy(
            src_ref=src, dst_ref=dst, send_sem=msend.at[index], recv_sem=mrecv.at[index],
            device_id={"grp": target}, device_id_type=MESH)

    fetches = [
        pltpu.make_async_copy(a, b, in_sem.at[k])
        for k, (a, b) in enumerate(((owners_hbm, owners), (offsets_hbm, offsets), (counts_hbm, counts),
                                    (working_hbm, working), (mixing_hbm, mixing), (strain_hbm, strain)))
    ]
    for fetch in fetches:
        fetch.start()
    barrier = pltpu.get_barrier_semaphore()

    @pl.when(is_end)
    def _():
        pl.semaphore_signal(barrier, inc=1, device_id={"grp": near}, device_id_type=MESH)

    @pl.when(jnp.logical_not(is_end))
    def _():
        for target in (end, far):
            pl.semaphore_signal(barrier, inc=1, device_id={"grp": target}, device_id_type=MESH)
        for target in flips:
            pl.semaphore_signal(barrier, inc=1, device_id={"seg": target}, device_id_type=MESH)

    for fetch in fetches:
        fetch.wait()
    live = jnp.where(working[...] > 0, counts[...], 0)
    high = live // 8
    row = lax.broadcasted_iota(jnp.int32, (META, n), 0)
    meta = jnp.where(row == 0, high, jnp.where(row == 1, live - 8 * high, 0)).astype(jnp.float32).astype(jnp.bfloat16)
    mext[:n] = mixing[...]
    mext[n:] = jnp.zeros((META, wide), jnp.bfloat16)
    mext[n:, :n] = meta
    own_counts = counts_column(meta, n)
    me = seg * (wide // n) + z
    chosen, picked = [], []
    for r in range(ROUNDS):
        row = lax.broadcasted_iota(jnp.int32, (SRC, wide), 0)
        column = lax.broadcasted_iota(jnp.int32, (SRC, wide), 1)
        place = (owners[r] - seg * (wide // n)) * n + offsets[r]
        picked.append(jnp.where(column == row + place, 1.0, 0.0))
        place = (owners[r] - me) * (2 * wide) + offsets[r]
        chosen.append(jnp.where(column[:, :n] == row[:, :n] + place, 1.0, 0.0))
    pick = jnp.concatenate(picked, axis=0).astype(jnp.bfloat16)
    chosen = jnp.concatenate(chosen, axis=0).astype(jnp.bfloat16)
    msel[:n] = jnp.dot(chosen, mixing[...], preferred_element_type=jnp.float32).astype(jnp.bfloat16)
    msel[n:] = jnp.zeros((META, wide), jnp.bfloat16)
    msel[n:, :n] = lax.dot_general(meta, chosen, NT, preferred_element_type=jnp.float32).astype(jnp.bfloat16)

    def usable(counts, c):
        position = lax.broadcasted_iota(jnp.int32, (n, edges[c + 1] - edges[c]), 1) + edges[c]
        return position.astype(jnp.float32) < counts

    def mask_own(c):
        part = jnp.where(usable(own_counts, c), strain[:, edges[c] : edges[c + 1]].astype(jnp.float32), 0.0)
        xall[pl.ds(z * n, n), edges[c] : edges[c + 1]] = part.astype(jnp.bfloat16)

    def energy(ref, c):
        part = ref[:n, edges[c] : edges[c + 1]].astype(jnp.float32)
        return jnp.sum(part * part, axis=1, keepdims=True)

    def whiten(out, ref, counts, total):
        gain = 1.0 / jnp.sqrt(total / jnp.maximum(counts, 1.0) + epsilon)
        for c in range(CHUNKS):
            part = ref[:n, edges[c] : edges[c + 1]].astype(jnp.float32)
            out[:, edges[c] : edges[c + 1]] = (part * gain).astype(jnp.bfloat16)

    @pl.when(is_end)
    def _():
        pl.semaphore_wait(barrier, 1)
        sends = []

        def go(c):
            sends.append(c)
            c.start()

        mask_own(0)
        go(x_copy(z, EX, 0, near))
        go(m_copy(msel, msel_end, 0, near))
        mask_own(1)
        go(x_copy(z, EX, 1, near))
        go(m_copy(mext, mext_end, 1, near))
        for c in range(2, CHUNKS):
            mask_own(c)
            go(x_copy(z, EX, c, near))
        w_total = s_total = jnp.zeros((n, 1), jnp.float32)
        for step in range(CHUNKS + 2):
            if step < CHUNKS:
                part_copy(fe, fe, FE, step, {"grp": near}).wait_recv()
                w_total += energy(fe, step)
            if step == CHUNKS - 1:
                whiten(w_out, fe, own_counts, w_total)
            if step >= 2:
                part_copy(s_all, s_all, SE, step - 2, {"grp": near}).wait_recv()
                s_total += energy(s_all, step - 2)
        whiten(s_out, s_all, counts_column(s_all[n:, :n], n), s_total)
        for c in sends:
            c.wait_send()

    @pl.when(jnp.logical_not(is_end))
    def _():
        pl.semaphore_wait(barrier, 5)
        sends = []

        def go(c):
            sends.append(c)
            c.start()

        def forward(c):
            x_copy(end, EX, c, end).wait_recv()
            go(x_copy(end, XE, c, far))

        def send_own(c):
            mask_own(c)
            go(x_copy(z, XI, c, far))

        send_own(0)
        send_own(1)
        forward(0)
        m_copy(msel_end, msel_end, 0, end).wait_recv()
        msel_sum[...] = msel[...] + msel_end[...]
        go(m_copy(msel_sum, msel_far, 2, far))
        forward(1)
        send_own(2)
        m_copy(mext_end, mext_end, 1, end).wait_recv()
        left[:n] = mext[:n]
        left[n : 2 * n] = mext_end[:n]
        end_counts = counts_column(mext_end[n:], n)
        m_copy(msel_far, msel_far, 2, far).wait_recv()
        left[2 * n : 3 * n] = msel_sum[:n] + msel_far[:n]
        left[3 * n :] = pick
        meta = msel_sum[n:] + msel_far[n:]
        src_counts = counts_column(meta, n)
        sa[n:] = jnp.zeros((META, samples), jnp.bfloat16)
        sa[n:, :n] = meta[:, :n]

        def process(c):
            a, b = edges[c], edges[c + 1]
            x_copy(far, XI, c, far).wait_recv()
            x_copy(far_end, XE, c, far).wait_recv()
            coupled = jnp.dot(left[...], xall[:, a:b], preferred_element_type=jnp.float32)
            own_x = xall[pl.ds(z * n, n), a:b].astype(jnp.float32)
            end_x = xall[pl.ds(end * n, n), a:b].astype(jnp.float32)
            fe[:, a:b] = jnp.where(usable(end_counts, c), end_x - coupled[n : 2 * n], 0.0).astype(jnp.bfloat16)
            part = jnp.where(usable(src_counts, c), coupled[3 * n :] - coupled[2 * n : 3 * n], 0.0)
            sa[:n, a:b] = part.astype(jnp.bfloat16)
            go(part_copy(sa, ra, SA, c, {"seg": flips[0]}))
            go(part_copy(fe, fe, FE, c, {"grp": end}))
            own = jnp.where(usable(own_counts, c), own_x - coupled[:n], 0.0)
            fown[:, a:b] = own
            return jnp.sum(own * own, axis=1, keepdims=True)

        def stage(mine, arrived, total, kind, c, flip):
            a, b = edges[c], edges[c + 1]
            part_copy(mine, arrived, kind, c, {"seg": flip}).wait_recv()
            total[:, a:b] = mine[:, a:b] + arrived[:, a:b]

        w_total = s_total = jnp.zeros((n, 1), jnp.float32)
        for step in range(CHUNKS + 3):
            if step + 2 < CHUNKS:
                forward(step + 2)
            if step + 3 < CHUNKS:
                send_own(step + 3)
            if step < CHUNKS:
                w_total += process(step)
            if 0 <= step - 1 < CHUNKS:
                stage(sa, ra, sb, SA, step - 1, flips[0])
                go(part_copy(sb, rb, SB, step - 1, {"seg": flips[1]}))
            if 0 <= step - 2 < CHUNKS:
                stage(sb, rb, sc, SB, step - 2, flips[1])
                go(part_copy(sc, rc, SC, step - 2, {"seg": flips[2]}))
            if 0 <= step - 3 < CHUNKS:
                stage(sc, rc, s_all, SC, step - 3, flips[2])
                go(part_copy(s_all, s_all, SE, step - 3, {"grp": end}))
                s_total += energy(s_all, step - 3)
            if step == CHUNKS:
                whiten(w_out, fown, own_counts, w_total)
        whiten(s_out, s_all, counts_column(s_all[n:, :n], n), s_total)
        for c in sends:
            c.wait_send()


def gather(strain, counts, working, mixing, owners, offsets):
    n, samples = strain.shape
    wide = mixing.shape[1]
    vmem = pl.BlockSpec(memory_space=pltpu.VMEM)
    part = pltpu.VMEM((n + META, samples), jnp.bfloat16)
    mat = pltpu.VMEM((n + META, wide), jnp.bfloat16)
    return pl.pallas_call(
        gather_kernel,
        out_shape=[jax.ShapeDtypeStruct((n, samples), jnp.bfloat16)] * 2,
        in_specs=[pl.BlockSpec(memory_space=pl.ANY)] * 6,
        out_specs=[vmem] * 2,
        scratch_shapes=[pltpu.SMEM((ROUNDS,), jnp.int32)] * 2 + [
            pltpu.VMEM((n, samples), jnp.bfloat16),
            pltpu.VMEM((1, n), jnp.int32),
            pltpu.VMEM((1, n), jnp.int32),
            pltpu.VMEM((n, wide), jnp.bfloat16),
            pltpu.SemaphoreType.DMA((6,)),
        ] + [mat] * 2 + [
            pltpu.VMEM((wide, samples), jnp.bfloat16),
            pltpu.VMEM((n, samples), jnp.float32),
            pltpu.VMEM((n, samples), jnp.bfloat16),
        ] + [part] * 7 + [mat] * 4 + [
            pltpu.VMEM((4 * n, wide), jnp.bfloat16),
            pltpu.SemaphoreType.DMA((8, CHUNKS)),
            pltpu.SemaphoreType.DMA((8, CHUNKS)),
            pltpu.SemaphoreType.DMA((3,)),
            pltpu.SemaphoreType.DMA((3,)),
        ],
        compiler_params=pltpu.CompilerParams(
            collective_id=0, has_side_effects=True, vmem_limit_bytes=56 * 1024 * 1024),
        name="gather",
    )(owners, offsets, strain, counts.reshape(1, n), working.reshape(1, n), mixing)


def gather_any(strain, counts, working, mixing, owners, offsets):
    positions = lax.broadcasted_iota(jnp.int32, strain.shape, 1)
    usable = (positions < counts[:, None]) & (working[:, None] > 0)
    masked = jnp.where(usable, strain, jnp.zeros_like(strain))
    coupled = jnp.dot(
        mixing,
        lax.all_gather(masked, "grp", axis=0, tiled=True),
        preferred_element_type=jnp.float32,
    )
    filtered = jnp.where(usable, masked.astype(jnp.float32) - coupled, jnp.float32(0.0))
    sumsq = jnp.sum(filtered * filtered, axis=1)
    spread = jnp.sqrt(sumsq / counts.astype(jnp.float32) + epsilon)
    whitened = (filtered / spread[:, None]).astype(jnp.bfloat16)
    me = lax.axis_index(("seg", "grp"))
    mine = [
        jnp.where(me == owners[r], lax.dynamic_slice_in_dim(whitened, offsets[r], SRC, 0), 0)
        for r in range(ROUNDS)
    ]
    sources = lax.psum(jnp.concatenate(mine, axis=0).astype(jnp.bfloat16), ("seg", "grp"))
    return whitened, sources


def on_device(strain, counts, working, mixing, owners, offsets):
    fits = lax.axis_size("seg") == 8 and lax.axis_size("grp") == 4
    whitened, sources = (gather if fits else gather_any)(strain, counts, working, mixing, owners, offsets)
    return correlate(whitened, sources)


def solution(mesh):
    in_specs = (
        P(("seg", "grp"), None),
        P(("seg", "grp")),
        P(("seg", "grp")),
        P("grp", None),
        P(),
        P(),
    )
    out_specs = P(None, None, None, ("seg", "grp"))
    return jax.shard_map(
        on_device, mesh=mesh, in_specs=in_specs, out_specs=out_specs, check_vma=False
    )
```

```python
import jax
import jax.numpy as jnp
from jax import lax
from jax.experimental import pallas as pl
from jax.experimental.pallas import tpu as pltpu
from jax.sharding import PartitionSpec as P

SRC = 64
LAG = 100
ROUNDS = 2
LAGS = 201
STEP = 10
GROUPS = LAG // STEP
PAD = 128

epsilon = 1e-05
NT = (((1,), (1,)), ((), ()))


def correlate_kernel(w_ref, s_ref, out_hbm, out_ref, wpad, spad, left, right, sem, in_sem):
    channels, samples = w_ref.shape
    rows = s_ref.shape[0]
    scale = 1.0 / float(samples) ** 0.5
    middle = pl.ds(PAD, samples)
    fetches = [
        pltpu.make_async_copy(ref, pad.at[:, middle], in_sem.at[k])
        for k, (pad, ref) in enumerate(((wpad, w_ref), (spad, s_ref)))
    ]
    for fetch in fetches:
        fetch.start()
    for pad in (wpad, spad):
        edge = jnp.zeros((pad.shape[0], PAD), pad.dtype)
        pad[:, :PAD] = edge
        pad[:, PAD + samples :] = edge
    for fetch in fetches:
        fetch.wait()
    half = STEP // 2

    def shift_sources(sign_index, group):
        start = PAD + (1 - 2 * sign_index) * STEP * group
        left[sign_index, group * rows : (group + 1) * rows, :] = spad[:, start : start + samples]

    def shift_pair(tile):
        for delta in (2 * (tile % half), 2 * (tile % half) + 1):
            start = PAD - (1 - 2 * (tile // half)) * (delta + 1)
            right[tile // half * STEP + delta] = wpad[:, start : start + samples]

    shift_pair(0)
    for group in range(GROUPS):
        shift_sources(0, group)

    centre = lax.dot_general(spad[:, middle], wpad[:, middle], NT, preferred_element_type=jnp.float32)
    centre = (centre * scale).astype(jnp.bfloat16)
    for r in range(ROUNDS):
        out_ref[r, LAG] = centre[r * SRC : (r + 1) * SRC]
        pltpu.make_async_copy(out_ref.at[r, LAG], out_hbm.at[r, LAG], sem).start()

    for tile in range(2 * half):
        sign_index, n = tile // half, tile % half
        if tile + 1 < 2 * half:
            shift_pair(tile + 1)
        if sign_index == 0:
            shift_sources(1, 2 * n)
            shift_sources(1, 2 * n + 1)
        pair = right[2 * tile : 2 * tile + 2].reshape(2 * channels, samples)
        products = lax.dot_general(left[sign_index], pair, NT, preferred_element_type=jnp.float32)
        products = (products * scale).astype(jnp.bfloat16)
        slabs = []
        for group in range(GROUPS):
            for r in range(ROUNDS):
                row = group * rows + r * SRC
                offset = STEP * group + 2 * n
                for d in range(2):
                    lag = LAG + (1 - 2 * sign_index) * (offset + d + 1)
                    out_ref[r, lag] = products[row : row + SRC, d * channels : (d + 1) * channels]
                slabs.append((r, pl.ds(LAG + offset + 1 if sign_index == 0 else LAG - offset - 2, 2)))
        for slab in slabs:
            pltpu.make_async_copy(out_ref.at[slab], out_hbm.at[slab], sem).start()
    pltpu.make_async_copy(out_ref, out_hbm, sem).wait()


def correlate(whitened, sources):
    channels, samples = whitened.shape
    rows = sources.shape[0]
    return pl.pallas_call(
        correlate_kernel,
        out_shape=jax.ShapeDtypeStruct((ROUNDS, LAGS, SRC, channels), jnp.bfloat16),
        in_specs=[pl.BlockSpec(memory_space=pl.ANY)] * 2,
        out_specs=pl.BlockSpec(memory_space=pl.ANY),
        scratch_shapes=[
            pltpu.VMEM((ROUNDS, LAGS, SRC, channels), jnp.bfloat16),
            pltpu.VMEM((channels, samples + 2 * PAD), jnp.bfloat16),
            pltpu.VMEM((rows, samples + 2 * PAD), jnp.bfloat16),
            pltpu.VMEM((2, GROUPS * rows, samples), jnp.bfloat16),
            pltpu.VMEM((2 * STEP, channels, samples), jnp.bfloat16),
            pltpu.SemaphoreType.DMA,
            pltpu.SemaphoreType.DMA((2,)),
        ],
        compiler_params=pltpu.CompilerParams(vmem_limit_bytes=56 * 1024 * 1024),
        cost_estimate=pl.CostEstimate(
            flops=2 * LAGS * rows * channels * samples, bytes_accessed=8 << 20, transcendentals=0
        ),
        name="correlate",
    )(whitened, sources)


EDGES = (0, 2, 4, 6, 8, 10, 11, 12, 13, 14)
CHUNKS = len(EDGES) - 1
META = 16
XI, XE, EX, FE, SA, SB, SC, SE = range(8)
MESH = pl.DeviceIdType.MESH


def counts_column(meta, n):
    lanes = meta[0:1, :n].astype(jnp.float32) * 8.0 + meta[1:2, :n].astype(jnp.float32)
    row = lax.broadcasted_iota(jnp.int32, (n, n), 0)
    lane = lax.broadcasted_iota(jnp.int32, (n, n), 1)
    return jnp.sum(jnp.where(row == lane, lanes, 0.0), axis=1, keepdims=True)


def gather_kernel(owners_hbm, offsets_hbm, strain_hbm, counts_hbm, working_hbm, mixing_hbm, w_out, s_out,
                  owners, offsets, strain, counts, working, mixing, in_sem, mext, msel, xall, fown, fe, sa, ra, sb, rb, sc, rc,
                  s_all, mext_end, msel_end, msel_sum, msel_far, left, send, recv, msend, mrecv):
    n, samples = strain.shape
    wide = mixing.shape[1]
    unit = samples // EDGES[-1]
    edges = [unit * e for e in EDGES]
    seg = lax.axis_index("seg")
    z = lax.axis_index("grp")
    is_end = (z % 3) == 0
    near = 1 + z // 3
    end = 3 * (z - 1)
    far = 3 - z
    far_end = 3 - end
    flips = [seg + 1 - 2 * (seg % 2), seg + 2 - 4 * ((seg // 2) % 2), seg + 4 - 8 * (seg // 4)]

    def cols(c):
        return pl.ds(edges[c], edges[c + 1] - edges[c])

    def copy(src, dst, kind, c, device):
        return pltpu.make_async_remote_copy(
            src_ref=src, dst_ref=dst, send_sem=send.at[kind, c], recv_sem=recv.at[kind, c],
            device_id=device, device_id_type=MESH)

    def block(index, c):
        return xall.at[pl.ds(index * n, n), cols(c)]

    def x_copy(index, kind, c, target):
        return copy(block(index, c), block(index, c), kind, c, {"grp": target})

    def part_copy(src, dst, kind, c, device):
        return copy(src.at[:, cols(c)], dst.at[:, cols(c)], kind, c, device)

    def m_copy(src, dst, index, target):
        return pltpu.make_async_remote_copy(
            src_ref=src, dst_ref=dst, send_sem=msend.at[index], recv_sem=mrecv.at[index],
            device_id={"grp": target}, device_id_type=MESH)

    fetches = [
        pltpu.make_async_copy(a, b, in_sem.at[k])
        for k, (a, b) in enumerate(((owners_hbm, owners), (offsets_hbm, offsets), (counts_hbm, counts),
                                    (working_hbm, working), (mixing_hbm, mixing), (strain_hbm, strain)))
    ]
    for fetch in fetches:
        fetch.start()
    barrier = pltpu.get_barrier_semaphore()

    @pl.when(is_end)
    def _():
        pl.semaphore_signal(barrier, inc=1, device_id={"grp": near}, device_id_type=MESH)

    @pl.when(jnp.logical_not(is_end))
    def _():
        for target in (end, far):
            pl.semaphore_signal(barrier, inc=1, device_id={"grp": target}, device_id_type=MESH)
        for target in flips:
            pl.semaphore_signal(barrier, inc=1, device_id={"seg": target}, device_id_type=MESH)

    for fetch in fetches:
        fetch.wait()
    live = jnp.where(working[...] > 0, counts[...], 0)
    high = live // 8
    row = lax.broadcasted_iota(jnp.int32, (META, n), 0)
    meta = jnp.where(row == 0, high, jnp.where(row == 1, live - 8 * high, 0)).astype(jnp.float32).astype(jnp.bfloat16)
    mext[:n] = mixing[...]
    mext[n:] = jnp.zeros((META, wide), jnp.bfloat16)
    mext[n:, :n] = meta
    own_counts = counts_column(meta, n)
    me = seg * (wide // n) + z
    chosen, picked = [], []
    for r in range(ROUNDS):
        row = lax.broadcasted_iota(jnp.int32, (SRC, wide), 0)
        column = lax.broadcasted_iota(jnp.int32, (SRC, wide), 1)
        place = (owners[r] - seg * (wide // n)) * n + offsets[r]
        picked.append(jnp.where(column == row + place, 1.0, 0.0))
        place = (owners[r] - me) * (2 * wide) + offsets[r]
        chosen.append(jnp.where(column[:, :n] == row[:, :n] + place, 1.0, 0.0))
    pick = jnp.concatenate(picked, axis=0).astype(jnp.bfloat16)
    chosen = jnp.concatenate(chosen, axis=0).astype(jnp.bfloat16)
    msel[:n] = jnp.dot(chosen, mixing[...], preferred_element_type=jnp.float32).astype(jnp.bfloat16)
    msel[n:] = jnp.zeros((META, wide), jnp.bfloat16)
    msel[n:, :n] = lax.dot_general(meta, chosen, NT, preferred_element_type=jnp.float32).astype(jnp.bfloat16)

    def usable(counts, c):
        position = lax.broadcasted_iota(jnp.int32, (n, edges[c + 1] - edges[c]), 1) + edges[c]
        return position.astype(jnp.float32) < counts

    def mask_own(c):
        part = jnp.where(usable(own_counts, c), strain[:, edges[c] : edges[c + 1]].astype(jnp.float32), 0.0)
        xall[pl.ds(z * n, n), edges[c] : edges[c + 1]] = part.astype(jnp.bfloat16)

    def energy(ref, c):
        part = ref[:n, edges[c] : edges[c + 1]].astype(jnp.float32)
        return jnp.sum(part * part, axis=1, keepdims=True)

    def whiten(out, ref, counts, total):
        gain = 1.0 / jnp.sqrt(total / jnp.maximum(counts, 1.0) + epsilon)
        for c in range(CHUNKS):
            part = ref[:n, edges[c] : edges[c + 1]].astype(jnp.float32)
            out[:, edges[c] : edges[c + 1]] = (part * gain).astype(jnp.bfloat16)

    @pl.when(is_end)
    def _():
        pl.semaphore_wait(barrier, 1)
        sends = []

        def go(c):
            sends.append(c)
            c.start()

        mask_own(0)
        go(x_copy(z, EX, 0, near))
        go(m_copy(msel, msel_end, 0, near))
        mask_own(1)
        go(x_copy(z, EX, 1, near))
        go(m_copy(mext, mext_end, 1, near))
        for c in range(2, CHUNKS):
            mask_own(c)
            go(x_copy(z, EX, c, near))
        w_total = s_total = jnp.zeros((n, 1), jnp.float32)
        for step in range(CHUNKS + 2):
            if step < CHUNKS:
                part_copy(fe, fe, FE, step, {"grp": near}).wait_recv()
                w_total += energy(fe, step)
            if step == CHUNKS - 1:
                whiten(w_out, fe, own_counts, w_total)
            if step >= 2:
                part_copy(s_all, s_all, SE, step - 2, {"grp": near}).wait_recv()
                s_total += energy(s_all, step - 2)
        whiten(s_out, s_all, counts_column(s_all[n:, :n], n), s_total)
        for c in sends:
            c.wait_send()

    @pl.when(jnp.logical_not(is_end))
    def _():
        pl.semaphore_wait(barrier, 5)
        sends = []

        def go(c):
            sends.append(c)
            c.start()

        def forward(c):
            x_copy(end, EX, c, end).wait_recv()
            go(x_copy(end, XE, c, far))

        def send_own(c):
            mask_own(c)
            go(x_copy(z, XI, c, far))

        send_own(0)
        send_own(1)
        forward(0)
        m_copy(msel_end, msel_end, 0, end).wait_recv()
        msel_sum[...] = msel[...] + msel_end[...]
        go(m_copy(msel_sum, msel_far, 2, far))
        forward(1)
        send_own(2)
        m_copy(mext_end, mext_end, 1, end).wait_recv()
        left[:n] = mext[:n]
        left[n : 2 * n] = mext_end[:n]
        end_counts = counts_column(mext_end[n:], n)
        m_copy(msel_far, msel_far, 2, far).wait_recv()
        left[2 * n : 3 * n] = msel_sum[:n] + msel_far[:n]
        left[3 * n :] = pick
        meta = msel_sum[n:] + msel_far[n:]
        src_counts = counts_column(meta, n)
        sa[n:] = jnp.zeros((META, samples), jnp.bfloat16)
        sa[n:, :n] = meta[:, :n]

        def process(c):
            a, b = edges[c], edges[c + 1]
            x_copy(far, XI, c, far).wait_recv()
            x_copy(far_end, XE, c, far).wait_recv()
            coupled = jnp.dot(left[...], xall[:, a:b], preferred_element_type=jnp.float32)
            own_x = xall[pl.ds(z * n, n), a:b].astype(jnp.float32)
            end_x = xall[pl.ds(end * n, n), a:b].astype(jnp.float32)
            fe[:, a:b] = jnp.where(usable(end_counts, c), end_x - coupled[n : 2 * n], 0.0).astype(jnp.bfloat16)
            part = jnp.where(usable(src_counts, c), coupled[3 * n :] - coupled[2 * n : 3 * n], 0.0)
            sa[:n, a:b] = part.astype(jnp.bfloat16)
            go(part_copy(sa, ra, SA, c, {"seg": flips[0]}))
            go(part_copy(fe, fe, FE, c, {"grp": end}))
            own = jnp.where(usable(own_counts, c), own_x - coupled[:n], 0.0)
            fown[:, a:b] = own
            return jnp.sum(own * own, axis=1, keepdims=True)

        def stage(mine, arrived, total, kind, c, flip):
            a, b = edges[c], edges[c + 1]
            part_copy(mine, arrived, kind, c, {"seg": flip}).wait_recv()
            total[:, a:b] = mine[:, a:b] + arrived[:, a:b]

        w_total = s_total = jnp.zeros((n, 1), jnp.float32)
        for step in range(CHUNKS + 3):
            if step + 2 < CHUNKS:
                forward(step + 2)
            if step + 3 < CHUNKS:
                send_own(step + 3)
            if step < CHUNKS:
                w_total += process(step)
            if 0 <= step - 1 < CHUNKS:
                stage(sa, ra, sb, SA, step - 1, flips[0])
                go(part_copy(sb, rb, SB, step - 1, {"seg": flips[1]}))
            if 0 <= step - 2 < CHUNKS:
                stage(sb, rb, sc, SB, step - 2, flips[1])
                go(part_copy(sc, rc, SC, step - 2, {"seg": flips[2]}))
            if 0 <= step - 3 < CHUNKS:
                stage(sc, rc, s_all, SC, step - 3, flips[2])
                go(part_copy(s_all, s_all, SE, step - 3, {"grp": end}))
                s_total += energy(s_all, step - 3)
            if step == CHUNKS:
                whiten(w_out, fown, own_counts, w_total)
        whiten(s_out, s_all, counts_column(s_all[n:, :n], n), s_total)
        for c in sends:
            c.wait_send()


def gather(strain, counts, working, mixing, owners, offsets):
    n, samples = strain.shape
    wide = mixing.shape[1]
    vmem = pl.BlockSpec(memory_space=pltpu.VMEM)
    part = pltpu.VMEM((n + META, samples), jnp.bfloat16)
    mat = pltpu.VMEM((n + META, wide), jnp.bfloat16)
    return pl.pallas_call(
        gather_kernel,
        out_shape=[jax.ShapeDtypeStruct((n, samples), jnp.bfloat16)] * 2,
        in_specs=[pl.BlockSpec(memory_space=pl.ANY)] * 6,
        out_specs=[vmem] * 2,
        scratch_shapes=[pltpu.SMEM((ROUNDS,), jnp.int32)] * 2 + [
            pltpu.VMEM((n, samples), jnp.bfloat16),
            pltpu.VMEM((1, n), jnp.int32),
            pltpu.VMEM((1, n), jnp.int32),
            pltpu.VMEM((n, wide), jnp.bfloat16),
            pltpu.SemaphoreType.DMA((6,)),
        ] + [mat] * 2 + [
            pltpu.VMEM((wide, samples), jnp.bfloat16),
            pltpu.VMEM((n, samples), jnp.float32),
            pltpu.VMEM((n, samples), jnp.bfloat16),
        ] + [part] * 7 + [mat] * 4 + [
            pltpu.VMEM((4 * n, wide), jnp.bfloat16),
            pltpu.SemaphoreType.DMA((8, CHUNKS)),
            pltpu.SemaphoreType.DMA((8, CHUNKS)),
            pltpu.SemaphoreType.DMA((3,)),
            pltpu.SemaphoreType.DMA((3,)),
        ],
        compiler_params=pltpu.CompilerParams(
            collective_id=0, has_side_effects=True, vmem_limit_bytes=56 * 1024 * 1024),
        name="gather",
    )(owners, offsets, strain, counts.reshape(1, n), working.reshape(1, n), mixing)


def gather_any(strain, counts, working, mixing, owners, offsets):
    positions = lax.broadcasted_iota(jnp.int32, strain.shape, 1)
    usable = (positions < counts[:, None]) & (working[:, None] > 0)
    masked = jnp.where(usable, strain, jnp.zeros_like(strain))
    coupled = jnp.dot(
        mixing,
        lax.all_gather(masked, "grp", axis=0, tiled=True),
        preferred_element_type=jnp.float32,
    )
    filtered = jnp.where(usable, masked.astype(jnp.float32) - coupled, jnp.float32(0.0))
    sumsq = jnp.sum(filtered * filtered, axis=1)
    spread = jnp.sqrt(sumsq / counts.astype(jnp.float32) + epsilon)
    whitened = (filtered / spread[:, None]).astype(jnp.bfloat16)
    me = lax.axis_index(("seg", "grp"))
    mine = [
        jnp.where(me == owners[r], lax.dynamic_slice_in_dim(whitened, offsets[r], SRC, 0), 0)
        for r in range(ROUNDS)
    ]
    sources = lax.psum(jnp.concatenate(mine, axis=0).astype(jnp.bfloat16), ("seg", "grp"))
    return whitened, sources


def on_device(strain, counts, working, mixing, owners, offsets):
    fits = lax.axis_size("seg") == 8 and lax.axis_size("grp") == 4
    whitened, sources = (gather if fits else gather_any)(strain, counts, working, mixing, owners, offsets)
    return correlate(whitened, sources)


def solution(mesh):
    in_specs = (
        P(("seg", "grp"), None),
        P(("seg", "grp")),
        P(("seg", "grp")),
        P("grp", None),
        P(),
        P(),
    )
    out_specs = P(None, None, None, ("seg", "grp"))
    return jax.shard_map(
        on_device, mesh=mesh, in_specs=in_specs, out_specs=out_specs, check_vma=False
    )
```
